256 devices in a mesh: ctx: 16 (over z, core), tp: 8 (over y, x_hi), grp: 2 (over x_lo).
Axes of the slice: x: 4 (x_hi: 2, x_lo: 2; x = x_hi * 2 + x_lo), y: 4, z: 8, core: 2. Of those that a mesh axis runs over, the one named last changes fastest.
Arguments:
- pre_q: bfloat16 [2, 4096, 8192], P('grp', 'ctx', 'tp')
- pre_k: bfloat16 [2, 4096, 1024], P('grp', 'ctx', 'tp')
- pre_v: bfloat16 [2, 4096, 1024], P('grp', 'ctx', 'tp'), may hold values from -6 to 6
- pre_ck: bfloat16 [2, 4096, 1024], P('grp', 'ctx', 'tp'), may hold values from -6 to 6
- pre_cv: bfloat16 [2, 4096, 1024], P('grp', 'ctx', 'tp'), may hold values from -6 to 6
- tract_offset: int32 [2], P('grp'), may hold values from 2048 to 4096
- owner: int32 [2, 4096, 1], P('grp', 'ctx'), may hold values from 0 to 15; in each aligned block of 256 rows (0 to 255, 256 to 511, ..., all dimensions but the last counted through in order) at most 32 rows name the same one
- tag: int32 [2, 4096], P('grp', 'ctx'), may hold values from 0 to 7
- out_weight: bfloat16 [8192, 8192], P('tp', 'ctx'), may hold values from -0.0625 to 0.0625
- dec_q: bfloat16 [2, 128, 2, 8192], P('grp', 'ctx', None, 'tp')
- dec_k: bfloat16 [2, 128, 2, 1024], P('grp', 'ctx', None, 'tp')
- dec_v: bfloat16 [2, 128, 2, 1024], P('grp', 'ctx', None, 'tp'), may hold values from -6 to 6
- dec_ck: bfloat16 [2, 128, 256, 1024], P('grp', 'ctx', None, 'tp'), may hold values from -6 to 6
- dec_cv: bfloat16 [2, 128, 256, 1024], P('grp', 'ctx', None, 'tp'), may hold values from -6 to 6
- cache_len: int32 [2, 128], P('grp', 'ctx'), may hold values from 1 to 256
Outputs:
- pre_out: bfloat16 [2, 4096, 8192], P('grp', 'tp', 'ctx')
- dec_out: bfloat16 [2, 128, 2, 8192], P('grp', 'ctx', None, 'tp')
The draws below stay inside these ranges and needn't reach their ends.
Inputs may be any that keep to these rules, and one draw needn't show every extreme that they name: Among the 256 stretch rows of one device at most 32 name the same owner, and exactly 32 do so on some device.
All inputs are finite; a program needn't handle non-finite values.
Results may differ from the reference program's by a relative error of at most 0.02.
Values may be sent and summed in bfloat16 or wider, within the bound.
A program may use at most 64 MiB of HBM per device.

```python
import math
import jax
import jax.numpy as jnp
import numpy as np
from jax import lax

QUERY_HEADS = 64
KEY_VALUE_HEADS = 8
HEAD_WIDTH = 128
STRETCH_DEV = 256
B_DEV = 8
CACHE_ROWS_MAX = 256
DECODE_STEPS = 2
D = 8192
KVW = 1024
STRETCH_TOKENS = 4096
PREFIX = 4096
DECODE_REQUESTS = 128
MOST = 32
N_CTX = 16


def shared_stretch_keys(key):
    base_offset = jnp.clip(jax.random.normal(jax.random.fold_in(key, 11), (2, STRETCH_TOKENS, KEY_VALUE_HEADS * HEAD_WIDTH), jnp.float32), -5.0, 5.0)
    rows = jnp.arange(STRETCH_TOKENS)
    paired = (rows % 97 == 4)[None, :, None]
    following = jnp.roll(base_offset, -1, axis=1)
    return jnp.where(paired, 0.99 * following, base_offset)


def shared_step_keys(key):
    base_offset = jnp.clip(jax.random.normal(jax.random.fold_in(key, 21), (2, DECODE_REQUESTS, DECODE_STEPS, KEY_VALUE_HEADS * HEAD_WIDTH), jnp.float32), -5.0, 5.0)
    rows = jnp.arange(DECODE_REQUESTS)
    paired = (rows % 5 == 0)[None, :, None, None] & (jnp.arange(DECODE_STEPS) == 1)[None, None, :, None]
    return jnp.where(paired, 0.99 * base_offset[:, :, 0:1, :], base_offset)


def draw_pre_k(key, part):
    return shared_stretch_keys(key).astype(jnp.bfloat16)


def draw_pre_q(key, part):
    key = jax.random.fold_in(key, 1)
    base_offset = jnp.clip(jax.random.normal(key, (2, STRETCH_TOKENS, QUERY_HEADS * HEAD_WIDTH), jnp.float32), -6.0, 6.0)
    return base_offset.astype(jnp.bfloat16)


def draw_dec_k(key, part):
    return shared_step_keys(key).astype(jnp.bfloat16)


def draw_dec_q(key, part):
    key = jax.random.fold_in(key, 2)
    base_offset = jnp.clip(jax.random.normal(key, (2, DECODE_REQUESTS, DECODE_STEPS, QUERY_HEADS * HEAD_WIDTH), jnp.float32), -6.0, 6.0)
    return base_offset.astype(jnp.bfloat16)


def set_ends(values, rng, least, top_value):
    place = [jax.random.randint(jax.random.fold_in(rng, axis), (), 0, length) for axis, length in enumerate(values.shape)]
    longest = values.shape.index(max(values.shape))
    beside = place[:longest] + [(place[longest] + 1) % values.shape[longest]] + place[longest + 1:]
    return values.at[tuple(place)].set(least).at[tuple(beside)].set(top_value)


def block_scale(own_key, extent, split, low, top_value):
    factor_of = 1.0
    for dim, shards_of in split:
        steps = jax.random.uniform(jax.random.fold_in(jax.random.fold_in(own_key, 6), dim), (shards_of,), jnp.float32, low / len(split), top_value / len(split))
        factor_of = factor_of * jnp.repeat(jnp.exp(steps), extent[dim] // shards_of).reshape((-1,) + (1,) * (len(extent) - 1 - dim))
    return factor_of


def assign_block(rng, own, number, rows, count, top, reach, skew):
    sequence = jax.random.permutation(rng, count)
    packed, usual = shares(count, rows * top, reach, skew, True), shares(count, rows * top, reach, skew, False)
    places = jnp.arange(count)

    def named(sizes, turn):
        used = int((sizes > 0).sum())
        fixed = max(1, used // 4)
        shifted = fixed + (places - fixed + turn * (used - fixed)) % max(1, count - fixed)
        return jnp.zeros((count,), jnp.int32).at[sequence[jnp.where(places < fixed, places, shifted)]].set(jnp.asarray(sizes, jnp.int32))

    sizes = jnp.where(number % 4 == 0, named(packed, number // 4), named(usual, number - number // 4 - 1))
    mixed = jax.random.permutation(jax.random.fold_in(own, 3), count)
    giver, sink = mixed[0:count // 2 * 2:2], mixed[1:count // 2 * 2:2]
    slack = jnp.minimum(sizes[giver] - 1, reach - sizes[sink]) // 2
    slack = jnp.where((giver == sequence[0]) | (sink == sequence[0]) | (sizes[sink] == 0), 0, jnp.maximum(slack, 0))
    shifted = jax.random.randint(jax.random.fold_in(own, 4), (count // 2,), 0, 1 << 20) % (slack + 1)
    sizes = sizes.at[giver].add(-shifted).at[sink].add(shifted)
    members = jnp.searchsorted(jnp.cumsum(sizes), jnp.arange(rows * top), side="right").astype(jnp.int32)
    table = members.reshape(top, rows).T
    table = table[jax.random.permutation(jax.random.fold_in(own, 1), rows)]
    turn = jax.random.randint(jax.random.fold_in(own, 2), (rows, 1), 0, top)
    return jnp.take_along_axis(table, (jnp.arange(top)[None, :] + turn) % top, axis=1)


def shares(amount, total, reach, lean, full):
    weights = [(1 << 20) // math.isqrt(grade ** lean) + 1 for grade in range(1, amount + 1)]
    largest = reach if full else min(reach, max(-(-total // amount), total * weights[0] // sum(weights)))
    least = 1 if total - largest >= amount - 1 else 0
    counts, spare = [largest] + [least] * (amount - 1), total - largest - least * (amount - 1)
    while spare > 0:
        movable = [i for i in range(1, amount) if counts[i] < largest] or [i for i in range(1, amount) if counts[i] < reach]
        whole, remaining = sum([weights[i] for i in movable]), spare
        for i in movable:
            extra = min(reach - counts[i], max(1, remaining * weights[i] // whole), spare)
            counts[i] = counts[i] + extra
            spare = spare - extra
    return np.array(counts)


def bell_draw(own_key, dims, width, most, shards=(), kind=jnp.bfloat16):
    values = jax.random.normal(own_key, dims, jnp.float32) * width
    if len(shards) > 0:
        values = block_scale(own_key, dims, shards, -0.22, 0.18) * values
    return jnp.clip(values, min=-most, max=most).astype(kind)


def setup_inputs(seed: int = 0) -> dict:
    seeds = jax.random.split(jax.random.key(seed), 16)
    pre_q = draw_pre_q(jax.random.fold_in(seeds[15], 71), 0)
    pre_k = draw_pre_k(jax.random.fold_in(seeds[15], 71), 0)
    pre_v = bell_draw(seeds[2], (2, STRETCH_TOKENS, KVW), 1.0, 6.0, ((0, 2), (1, 16), (2, 8)))
    pre_ck = bell_draw(seeds[3], (2, PREFIX, KVW), 1.0, 6.0, ((0, 2), (1, 16), (2, 8)))
    pre_cv = bell_draw(seeds[4], (2, PREFIX, KVW), 1.0, 6.0, ((0, 2), (1, 16), (2, 8)))
    tract_offset = jax.random.randint(seeds[5], (2,), PREFIX // 2, PREFIX + 1).astype(jnp.int32)
    owner_keys = jax.random.split(jax.random.fold_in(seeds[6], 1), 2 * STRETCH_TOKENS // STRETCH_DEV)
    owner_turns = jax.random.permutation(jax.random.fold_in(seeds[6], 3), 2 * STRETCH_TOKENS // STRETCH_DEV)
    owner = jax.vmap(lambda own, number: assign_block(jax.random.fold_in(seeds[6], 2), own, number, STRETCH_DEV, N_CTX, 1, MOST, 2))(owner_keys, owner_turns).reshape((2, STRETCH_TOKENS, 1))
    tag = set_ends(jax.random.randint(seeds[7], (2, STRETCH_TOKENS), 0, B_DEV), jax.random.fold_in(seeds[7], 1), 0, B_DEV - 1).astype(jnp.int32)
    out_weight = bell_draw(seeds[8], (D, D), D ** -0.5, 0.0625, ((0, 8), (1, 16)))
    dec_q = draw_dec_q(jax.random.fold_in(seeds[15], 71), 0)
    dec_k = draw_dec_k(jax.random.fold_in(seeds[15], 71), 0)
    dec_v = bell_draw(seeds[11], (2, DECODE_REQUESTS, DECODE_STEPS, KVW), 1.0, 6.0, ((0, 2), (1, 16), (3, 8)))
    dec_ck = bell_draw(seeds[12], (2, DECODE_REQUESTS, CACHE_ROWS_MAX, KVW), 1.0, 6.0, ((0, 2), (1, 16), (3, 8)))
    dec_cv = bell_draw(seeds[13], (2, DECODE_REQUESTS, CACHE_ROWS_MAX, KVW), 1.0, 6.0, ((0, 2), (1, 16), (3, 8)))
    cache_len = set_ends(jax.random.randint(seeds[14], (2, DECODE_REQUESTS), 1, CACHE_ROWS_MAX + 1), jax.random.fold_in(seeds[14], 1), 1, CACHE_ROWS_MAX).astype(jnp.int32)
    return dict(pre_q=pre_q, pre_k=pre_k, pre_v=pre_v, pre_ck=pre_ck, pre_cv=pre_cv, tract_offset=tract_offset, owner=owner, tag=tag, out_weight=out_weight, dec_q=dec_q, dec_k=dec_k, dec_v=dec_v, dec_ck=dec_ck, dec_cv=dec_cv, cache_len=cache_len)


def prefill_part(query_rows, rows_of_keys, rows_of_values, prefix_key_rows, prefix_value_rows, prefix_live):
    group_of_heads = QUERY_HEADS // KEY_VALUE_HEADS
    count_of_keys = PREFIX + STRETCH_TOKENS
    every_key_row = jnp.concatenate([prefix_key_rows, rows_of_keys], 0).astype(jnp.float32).reshape(count_of_keys, KEY_VALUE_HEADS, HEAD_WIDTH)
    every_value_row = jnp.concatenate([prefix_value_rows, rows_of_values], 0).astype(jnp.float32).reshape(count_of_keys, KEY_VALUE_HEADS, HEAD_WIDTH)
    positions = jnp.arange(count_of_keys, dtype=jnp.int32)
    heads_of_query = query_rows.astype(jnp.float32).reshape(STRETCH_TOKENS, KEY_VALUE_HEADS, group_of_heads, HEAD_WIDTH)
    block_rows = math.gcd(STRETCH_TOKENS, 64)
    score_scale = HEAD_WIDTH ** -0.5

    def one_block(first_row):
        query_block = lax.dynamic_slice_in_dim(heads_of_query, first_row, block_rows, 0)
        rows_now = first_row + jnp.arange(block_rows, dtype=jnp.int32)
        visible = jnp.where(positions[None, :] < PREFIX, positions[None, :] < prefix_live,
                            positions[None, :] - PREFIX <= rows_now[:, None])
        scores = jnp.einsum("qhgd,khd->hgqk", query_block, every_key_row) * score_scale
        scores = jnp.where(visible[None, None], scores, -jnp.inf)
        row_max = jnp.max(scores, axis=-1, keepdims=True)
        weight_rows = jnp.exp(scores - row_max)
        row_total = jnp.sum(weight_rows, axis=-1)
        rounded = lax.optimization_barrier(weight_rows.astype(jnp.bfloat16))
        weighted = jnp.einsum("hgqk,khd->qhgd", rounded.astype(jnp.float32), every_value_row)
        result = weighted / jnp.transpose(row_total, (2, 0, 1))[..., None]
        return result.reshape(block_rows, D).astype(jnp.bfloat16)

    block_starts = jnp.arange(0, STRETCH_TOKENS, block_rows, dtype=jnp.int32)
    return lax.map(one_block, block_starts).reshape(STRETCH_TOKENS, D)


def decode_part(query_rows, newest_keys, newest_values, keys_in_cache, values_in_cache, keys_handed_over, values_handed_over, request_of_row, live_rows):
    group_of_heads = QUERY_HEADS // KEY_VALUE_HEADS
    score_scale = HEAD_WIDTH ** -0.5
    heads_of_query = query_rows.astype(jnp.float32).reshape(DECODE_REQUESTS, DECODE_STEPS, KEY_VALUE_HEADS, group_of_heads, HEAD_WIDTH)
    cached_key_rows = keys_in_cache.astype(jnp.float32).reshape(DECODE_REQUESTS, CACHE_ROWS_MAX, KEY_VALUE_HEADS, HEAD_WIDTH)
    cached_value_rows = values_in_cache.astype(jnp.float32).reshape(DECODE_REQUESTS, CACHE_ROWS_MAX, KEY_VALUE_HEADS, HEAD_WIDTH)
    handed_key_rows = keys_handed_over.astype(jnp.float32).reshape(STRETCH_TOKENS, KEY_VALUE_HEADS, HEAD_WIDTH)
    handed_value_rows = values_handed_over.astype(jnp.float32).reshape(STRETCH_TOKENS, KEY_VALUE_HEADS, HEAD_WIDTH)
    fresh_key_rows = newest_keys.astype(jnp.float32).reshape(DECODE_REQUESTS, DECODE_STEPS, KEY_VALUE_HEADS, HEAD_WIDTH)
    fresh_value_rows = newest_values.astype(jnp.float32).reshape(DECODE_REQUESTS, DECODE_STEPS, KEY_VALUE_HEADS, HEAD_WIDTH)
    cache_mask = jnp.arange(CACHE_ROWS_MAX, dtype=jnp.int32)[None, :] < live_rows[:, None]
    hand_mask = request_of_row[None, :] == jnp.arange(DECODE_REQUESTS, dtype=jnp.int32)[:, None]
    fresh_mask = jnp.arange(DECODE_STEPS)[None, :] <= jnp.arange(DECODE_STEPS)[:, None]
    score_cache = jnp.einsum("rskgd,rckd->rskgc", heads_of_query, cached_key_rows) * score_scale
    score_cache = jnp.where(cache_mask[:, None, None, None, :], score_cache, -jnp.inf)
    score_hand = jnp.einsum("rskgd,hkd->rskgh", heads_of_query, handed_key_rows) * score_scale
    score_hand = jnp.where(hand_mask[:, None, None, None, :], score_hand, -jnp.inf)
    score_fresh = jnp.einsum("rskgd,rtkd->rskgt", heads_of_query, fresh_key_rows) * score_scale
    score_fresh = jnp.where(fresh_mask[None, :, None, None, :], score_fresh, -jnp.inf)
    scores = jnp.concatenate([score_cache, score_hand, score_fresh], axis=-1)
    row_max = jnp.max(scores, axis=-1, keepdims=True)
    weight_rows = jnp.exp(scores - row_max)
    row_total = jnp.sum(weight_rows, axis=-1, keepdims=True)
    rounded = lax.optimization_barrier(weight_rows.astype(jnp.bfloat16)).astype(jnp.float32)
    part_cache = rounded[..., :CACHE_ROWS_MAX]
    part_hand = rounded[..., CACHE_ROWS_MAX:CACHE_ROWS_MAX + STRETCH_TOKENS]
    part_fresh = rounded[..., CACHE_ROWS_MAX + STRETCH_TOKENS:]
    weighted = jnp.einsum("rskgc,rckd->rskgd", part_cache, cached_value_rows)
    weighted = weighted + jnp.einsum("rskgh,hkd->rskgd", part_hand, handed_value_rows)
    weighted = weighted + jnp.einsum("rskgt,rtkd->rskgd", part_fresh, fresh_value_rows)
    result = weighted / row_total
    return result.reshape(DECODE_REQUESTS, DECODE_STEPS, D).astype(jnp.bfloat16)


def reference(pre_q, pre_k, pre_v, pre_ck, pre_cv, tract_offset, owner, tag, out_weight, dec_q, dec_k, dec_v, dec_ck, dec_cv, cache_len):
    prefill_outs = []
    decode_outs = []
    for pool_index in range(2):
        attended = prefill_part(pre_q[pool_index], pre_k[pool_index], pre_v[pool_index],
                                pre_ck[pool_index], pre_cv[pool_index], tract_offset[pool_index])
        projected = jnp.dot(attended, out_weight, preferred_element_type=jnp.float32)
        prefill_outs.append(projected.astype(jnp.bfloat16))
        source_pool = 1 - pool_index
        request_of_row = (owner[source_pool, :, 0] * B_DEV + tag[source_pool]).astype(jnp.int32)
        decode_outs.append(decode_part(dec_q[pool_index], dec_k[pool_index], dec_v[pool_index],
                                       dec_ck[pool_index], dec_cv[pool_index],
                                       pre_k[source_pool], pre_v[source_pool], request_of_row,
                                       cache_len[pool_index]))
    return jnp.stack(prefill_outs), jnp.stack(decode_outs)
```

```python
import jax
import jax.numpy as jnp
from jax import lax
from jax.experimental import pallas as pl
from jax.experimental.pallas import tpu as pltpu
from jax.sharding import PartitionSpec as P

HEAD = 128
HEADS = 8
ROWS = 256
CHIPS = 8
TP = 8
PIECE = 64
NEG = -1e30
C2 = 128**-0.5 * 1.4426950408889634
F32, BF16 = jnp.float32, jnp.bfloat16
MESH = pl.DeviceIdType.MESH
NT = (((1,), (1,)), ((), ()))
NN = (((1,), (0,)), ((), ()))

CK, CV, SK, SV, LB, PACK = 0, 256, 512, 768, 1024, 1040


def dot(a, b, dims):
    return lax.dot_general(a, b, dims, preferred_element_type=F32)


def kernel(
    off_ref, len_ref, q_hbm, k_hbm, v_hbm, ck_hbm, cv_hbm, lab_hbm, w_hbm,
    dq_hbm, dk_hbm, dv_hbm, dck_hbm, dcv_hbm,
    out_ref, dec_ref,
    kv, q_s, v_s, w_s, dq_s, dqs, dk_s, dv_s, dck_s, dcv_s,
    m_s, l_s, acc_s, abuf, pbuf, rbuf, sbuf, obuf, dqp, hand, handin,
    lsem, ksend, krecv, ksibs, ksibr, asend, arecv, asibs, asibr,
    psend, precv, osend, orecv, dsend, drecv, hsend, hrecv,
):
    c = lax.axis_index("ctx")
    t = lax.axis_index("tp")
    g = lax.axis_index("grp")
    z = c // 2
    core = lax.rem(c, 2)
    right = (lax.rem(c + 2, 16), t, g)
    left = (lax.rem(c + 14, 16), t, g)
    sib = (c + 1 - 2 * core, t, g)
    other = (c, t, 1 - g)

    def chip(n):
        return lax.rem(n + CHIPS, CHIPS)

    def local(i, src, dst):
        return pltpu.make_async_copy(src, dst, lsem.at[i])

    def remote(src, dst, send, recv, device):
        return pltpu.make_async_remote_copy(
            src_ref=src, dst_ref=dst, send_sem=send, recv_sem=recv, device_id=device, device_id_type=MESH
        )

    mine = kv.at[z, core]
    ins = [
        local(0, ck_hbm, mine.at[pl.ds(CK, 256)]),
        local(1, k_hbm, mine.at[pl.ds(SK, 256)]),
        local(2, lab_hbm, mine.at[pl.ds(LB, 16)]),
        local(3, cv_hbm, v_s.at[0]),
        local(4, v_hbm, v_s.at[1]),
        local(5, dq_hbm, dq_s),
        local(6, q_hbm, q_s),
        local(7, w_hbm, w_s),
        local(8, dck_hbm, dck_s),
        local(9, dcv_hbm, dcv_s),
        local(10, dk_hbm, dk_s),
        local(11, dv_hbm, dv_s),
    ]
    for cp in ins:
        cp.start()

    barrier = pltpu.get_barrier_semaphore()
    for device in (right, left, sib, other):
        pl.semaphore_signal(barrier, inc=1, device_id=device, device_id_type=MESH)

    def greet(j, _):
        pl.semaphore_signal(barrier, inc=1, device_id=(c, lax.rem(t + 1 + j, TP), g), device_id_type=MESH)
        return 0

    lax.fori_loop(0, TP - 1, greet, 0)

    for i in range(6):
        ins[i].wait()
    for i, base in ((0, CV), (1, SV)):
        vt = v_s[i].astype(F32).T.astype(BF16)
        kv[z, core, base : base + 128, :] = vt[:, :128]
        kv[z, core, base + 128 : base + 256, :] = vt[:, 128:]
    for h in range(HEADS):
        dqs[h * 16 : (h + 1) * 16, :] = dq_s[:, h * HEAD : (h + 1) * HEAD]
    m_s[...] = jnp.full_like(m_s, NEG)
    l_s[...] = jnp.zeros_like(l_s)
    acc_s[...] = jnp.zeros_like(acc_s)

    pl.semaphore_wait(barrier, 4 + TP - 1)

    def ring_right(buf, sems, rsems, n, step):
        return remote(buf.at[n, core], buf.at[n, core], sems.at[0, step], rsems.at[0, step], right)

    def ring_left(buf, sems, rsems, n, step):
        return remote(buf.at[n, core], buf.at[n, core], sems.at[1, step], rsems.at[1, step], left)

    def to_sib(buf, sems, rsems, n):
        return remote(buf.at[n, core], buf.at[n, core], sems.at[n], rsems.at[n], sib)

    def from_sib(buf, sems, rsems, n):
        return remote(buf.at[n, 1 - core], buf.at[n, 1 - core], sems.at[n], rsems.at[n], sib)

    def last_right(buf, sems, rsems, n, rows, first):
        part = buf.at[n, core, pl.ds(first, rows)]
        return remote(part, part, sems.at[0, 3], rsems.at[0, 3], right)

    def last_left(buf, sems, rsems, n, rows, first):
        part = buf.at[n, core, pl.ds(first, rows)]
        return remote(part, part, sems.at[1, 3], rsems.at[1, 3], left)

    kvr = (kv, ksend, krecv)
    kvs = (kv, ksibs, ksibr)
    dq_copy = remote(dqs, dqp, dsend, drecv, other)

    ring_right(*kvr, z, 0).start()
    ring_left(*kvr, z, 0).start()
    to_sib(*kvs, z).start()
    dq_copy.start()
    ins[6].wait()

    def values_of(n, k, base):
        return jnp.concatenate([kv[n, k, base : base + 128, :], kv[n, k, base + 128 : base + 256, :]], axis=1)

    key_row = lax.broadcasted_iota(jnp.int32, (256, 256), 0)
    query_col = lax.broadcasted_iota(jnp.int32, (256, 256), 1)

    def attend(blocks):
        def scores(h):
            q = q_s[:, h * HEAD : (h + 1) * HEAD]
            return [dot(kv[n, k, kb : kb + 256, :], q, NT) for n, k, kb, _, _ in blocks]

        following = scores(0)
        for h in range(HEADS):
            ss = following
            if h < HEADS - 1:
                following = scores(h + 1)
            ss = [s if b[4] is None else jnp.where(b[4], s, -jnp.inf) for s, b in zip(ss, blocks)]
            top = ss[0]
            for s in ss[1:]:
                top = jnp.maximum(top, s)
            before = m_s[h]
            now = jnp.maximum(before, jnp.max(top, axis=0, keepdims=True))
            rescale = jnp.exp2((before - now) * C2)
            shift = now * C2
            total = None
            acc = acc_s[h] * rescale
            for s, (n, k, _, vb, _) in zip(ss, blocks):
                p = jnp.exp2(s * C2 - shift)
                total = p if total is None else total + p
                acc = acc + dot(values_of(n, k, vb), p.astype(BF16), NN)
            m_s[h] = now
            l_s[h] = l_s[h] * rescale + jnp.sum(total, axis=0, keepdims=True)
            acc_s[h] = acc

    def prefix(n):
        live = off_ref[0]
        return [(n, k, CK, CV, key_row < live - (2 * n + k) * 256) for k in (0, 1)]

    def stretch(n):
        return [(n, k, SK, SV, None) for k in (0, 1)]

    def diagonal():
        return [(z, k, SK, SV, key_row + (k - core) * 256 <= query_col) for k in (0, 1)]

    def visible(k):
        @pl.when((z >= k) & (z + k >= CHIPS))
        def _():
            attend(stretch(z - k) + stretch(z + k - CHIPS))

        @pl.when((z >= k) & (z + k < CHIPS))
        def _():
            attend(stretch(z - k))

    from_sib(*kvs, z).wait_recv()
    attend(prefix(z) + diagonal())

    def kv_step(k, _):
        before, after = chip(z - k), chip(z + k)
        ring_right(*kvr, before, k - 1).wait_recv()
        ring_left(*kvr, after, k - 1).wait_recv()

        @pl.when(k < 3)
        def _():
            ring_right(*kvr, before, k).start()
            ring_left(*kvr, after, k).start()

        @pl.when(k == 3)
        def _():
            last_right(*kvr, before, SK, 0).start()
            last_left(*kvr, after, PACK - SK, SK).start()

        to_sib(*kvs, before).start()
        to_sib(*kvs, after).start()

        @pl.when(k > 1)
        def _():
            visible(k - 1)

        from_sib(*kvs, before).wait_recv()
        from_sib(*kvs, after).wait_recv()
        attend(prefix(before) + prefix(after))
        return 0

    lax.fori_loop(1, 4, kv_step, 0)
    far = chip(z + 4)
    last_right(*kvr, far, SK, 0).wait_recv()
    last_left(*kvr, far, PACK - SK, SK).wait_recv()
    to_sib(*kvs, far).start()
    visible(3)
    from_sib(*kvs, far).wait_recv()
    attend(prefix(far))

    @pl.when(z >= 4)
    def _():
        attend(stretch(z - 4))

    for h in range(HEADS):
        rows = (acc_s[h] / l_s[h]).T
        abuf[z, core, :, h * HEAD : (h + 1) * HEAD] = rows.astype(BF16)

    atr = (abuf, asend, arecv)
    ats = (abuf, asibs, asibr)
    ring_right(*atr, z, 0).start()
    ring_left(*atr, z, 0).start()
    to_sib(*ats, z).start()
    ins[7].wait()

    def piece_out(n, j):
        to = lax.rem(t + 1 + j, TP)
        return remote(
            pbuf.at[n, pl.ds(to * PIECE, PIECE)], rbuf.at[n, t], psend.at[n, to], precv.at[n, t], (c, to, g)
        )

    def piece_in(n, j):
        of = lax.rem(t + 1 + j, TP)
        return remote(
            pbuf.at[n, pl.ds(of * PIECE, PIECE)], rbuf.at[n, of], psend.at[n, of], precv.at[n, of], (c, of, g)
        )

    def project(n):
        def one(k, _):
            pbuf[n, pl.ds(pl.multiple_of(k * 256, 256), 256), :] = dot(abuf[n, k], w_s[...], NN).astype(BF16)
            return 0

        lax.fori_loop(0, 2, one, 0)

        def send(j, _):
            piece_out(n, j).start()
            return 0

        lax.fori_loop(0, TP - 1, send, 0)

    def collect(n):
        def arrive(j, _):
            piece_in(n, j).wait_recv()
            return 0

        lax.fori_loop(0, TP - 1, arrive, 0)
        total = pbuf[n, pl.ds(pl.multiple_of(t * PIECE, PIECE), PIECE), :].astype(F32)
        for j in range(TP - 1):
            total = total + rbuf[n, lax.rem(t + 1 + j, TP)].astype(F32)

        @pl.when(n == t)
        def _():
            obuf[t] = total.astype(BF16)

        @pl.when(n != t)
        def _():
            sbuf[n] = total.astype(BF16)
            remote(sbuf.at[n], obuf.at[t], osend.at[n], orecv.at[t], (c, n, g)).start()

    row_id = lax.broadcasted_iota(jnp.int32, (128, 256), 0)
    col_id = lax.broadcasted_iota(jnp.int32, (128, 256), 1)
    request = lax.rem(row_id, 16) // 2
    initial = (jnp.full((128, 1), NEG, F32), jnp.zeros((128, 1), F32), jnp.zeros((128, HEAD), F32))

    def fold(state, parts):
        m, l, acc = state
        now = m
        for s, _ in parts:
            now = jnp.maximum(now, jnp.max(s, axis=1, keepdims=True))
        rescale = jnp.exp2((m - now) * C2)
        l = l * rescale
        acc = acc * rescale
        for s, weigh in parts:
            p = jnp.exp2((s - now) * C2)
            l = l + jnp.sum(p, axis=1, keepdims=True)
            acc = acc + weigh(p.astype(BF16))
        return now, l, acc

    def hand_over():
        wanted = (request + c * 8).astype(F32)

        def one(n, state):
            parts = []
            for k in (0, 1):
                labels = kv[n, k, LB : LB + 16, :].astype(F32)
                label = jnp.concatenate([labels[0:1], labels[1:2]], axis=1)
                s = dot(dqp[...], kv[n, k, SK : SK + 256, :], NT)
                s = jnp.where(label == wanted, s, -jnp.inf)
                parts.append((s, lambda p, k=k: dot(p, values_of(n, k, SV), NT)))
            return fold(state, parts)

        m, l, acc = lax.fori_loop(0, CHIPS, one, initial)
        hand[:, 0:128] = acc
        hand[:, 128:256] = jnp.broadcast_to(m, (128, 128))
        hand[:, 256:384] = jnp.broadcast_to(l, (128, 128))

    def cached():
        def one(i, state):
            parts = []
            for k in (0, 1):
                r = 2 * i + k
                rows = pl.ds(pl.multiple_of(r * 256, 256), 256)
                s = dot(dqs[...], dck_s[rows, :], NT)
                s = jnp.where((request == r) & (col_id < len_ref[r]), s, -jnp.inf)
                parts.append((s, lambda p, rows=rows: dot(p, dcv_s[rows, :], NN)))
            return fold(state, parts)

        state = lax.fori_loop(0, 4, one, initial)
        rows16 = lax.broadcasted_iota(jnp.int32, (128, 16), 0)
        cols16 = lax.broadcasted_iota(jnp.int32, (128, 16), 1)
        seen = (lax.rem(rows16, 16) // 2 == cols16 // 2) & (lax.rem(cols16, 2) <= lax.rem(rows16, 2))
        s = jnp.where(seen, dot(dqs[...], dk_s[...], NT), -jnp.inf)
        return fold(state, [(s, lambda p: dot(p, dv_s[...], NN))])

    hand_copy = remote(hand, handin, hsend, hrecv, other)

    from_sib(*ats, z).wait_recv()
    project(z)

    def at_step(k, _):
        before, after = chip(z - k), chip(z + k)
        ring_right(*atr, before, k - 1).wait_recv()
        ring_left(*atr, after, k - 1).wait_recv()

        @pl.when(k < 3)
        def _():
            ring_right(*atr, before, k).start()
            ring_left(*atr, after, k).start()

        @pl.when(k == 3)
        def _():
            last_right(*atr, before, 128, 0).start()
            last_left(*atr, after, 128, 128).start()

        to_sib(*ats, before).start()
        to_sib(*ats, after).start()

        @pl.when(k == 1)
        def _():
            collect(z)

        @pl.when(k > 1)
        def _():
            collect(chip(z - k + 1))
            collect(chip(z + k - 1))

        from_sib(*ats, before).wait_recv()
        from_sib(*ats, after).wait_recv()
        project(before)
        project(after)

        @pl.when(k == 1)
        def _():
            dq_copy.wait_recv()
            hand_over()
            hand_copy.start()

        return 0

    lax.fori_loop(1, 4, at_step, 0)
    for i in range(8, 12):
        ins[i].wait()
    own = cached()
    last_right(*atr, far, 128, 0).wait_recv()
    last_left(*atr, far, 128, 128).wait_recv()
    to_sib(*ats, far).start()
    collect(chip(z - 3))
    collect(chip(z + 3))
    from_sib(*ats, far).wait_recv()
    project(far)

    hand_copy.wait_recv()
    m, l, acc = own
    m_h, l_h = handin[:, 128:129], handin[:, 256:257]
    top = jnp.maximum(m, m_h)
    a, b = jnp.exp2((m - top) * C2), jnp.exp2((m_h - top) * C2)
    result = (acc * a + handin[:, 0:128] * b) / (l * a + l_h * b)
    for h in range(HEADS):
        dec_ref[:, h * HEAD : (h + 1) * HEAD] = result[h * 16 : (h + 1) * 16].astype(BF16)

    collect(far)

    def finish(j, _):
        of = lax.rem(t + 1 + j, TP)
        remote(sbuf.at[of], obuf.at[of], osend.at[of], orecv.at[of], (c, of, g)).wait_recv()
        return 0

    lax.fori_loop(0, TP - 1, finish, 0)
    for j in range(TP):
        out_ref[j * PIECE : (j + 1) * PIECE, :] = obuf[j]

    dq_copy.wait_send()
    hand_copy.wait_send()
    for buf, sends, recvs, sibs, sibr, rows in (
        (kv, ksend, krecv, ksibs, ksibr, (SK, 0, PACK - SK, SK)),
        (abuf, asend, arecv, asibs, asibr, (128, 0, 128, 128)),
    ):

        def sent(k, _, buf=buf, sends=sends, recvs=recvs):
            ring_right(buf, sends, recvs, chip(z - k), k).wait_send()
            ring_left(buf, sends, recvs, chip(z + k), k).wait_send()
            return 0

        lax.fori_loop(0, 3, sent, 0)
        last_right(buf, sends, recvs, chip(z - 3), rows[0], rows[1]).wait_send()
        last_left(buf, sends, recvs, chip(z + 3), rows[2], rows[3]).wait_send()

        def passed(n, _, buf=buf, sibs=sibs, sibr=sibr):
            to_sib(buf, sibs, sibr, n).wait_send()
            return 0

        lax.fori_loop(0, CHIPS, passed, 0)

    def pieces(n, _):
        def one(j, _):
            piece_out(n, j).wait_send()
            return 0

        lax.fori_loop(0, TP - 1, one, 0)

        @pl.when(n != t)
        def _():
            remote(sbuf.at[n], obuf.at[t], osend.at[n], orecv.at[t], (c, n, g)).wait_send()

        return 0

    lax.fori_loop(0, CHIPS, pieces, 0)


def shards(
    pre_q, pre_k, pre_v, pre_ck, pre_cv, tract_offset, owner, tag, out_weight,
    dec_q, dec_k, dec_v, dec_ck, dec_cv, cache_len,
):
    label = (owner[0, :, 0] * 8 + tag[0]).astype(BF16).reshape(2, 128)
    label = jnp.pad(label, ((0, 14), (0, 0)))
    vmem, dma = pltpu.VMEM, pltpu.SemaphoreType.DMA
    anywhere = pl.BlockSpec(memory_space=pl.ANY)
    smem = pl.BlockSpec(memory_space=pltpu.SMEM)
    whole = pl.BlockSpec(memory_space=pltpu.VMEM)
    out, dec = pl.pallas_call(
        kernel,
        out_shape=(jax.ShapeDtypeStruct((512, 512), BF16), jax.ShapeDtypeStruct((16, 1024), BF16)),
        in_specs=[smem, smem] + [anywhere] * 12,
        out_specs=(whole, whole),
        scratch_shapes=[
            vmem((CHIPS, 2, PACK, HEAD), BF16),
            vmem((ROWS, 1024), BF16),
            vmem((2, ROWS, HEAD), BF16),
            vmem((1024, 512), BF16),
            vmem((16, 1024), BF16),
            vmem((128, HEAD), BF16),
            vmem((16, HEAD), BF16),
            vmem((16, HEAD), BF16),
            vmem((2048, HEAD), BF16),
            vmem((2048, HEAD), BF16),
            vmem((HEADS, 1, ROWS), F32),
            vmem((HEADS, 1, ROWS), F32),
            vmem((HEADS, HEAD, ROWS), F32),
            vmem((CHIPS, 2, ROWS, 1024), BF16),
            vmem((CHIPS, 512, 512), BF16),
            vmem((CHIPS, TP, PIECE, 512), BF16),
            vmem((CHIPS, PIECE, 512), BF16),
            vmem((TP, PIECE, 512), BF16),
            vmem((128, HEAD), BF16),
            vmem((128, 384), F32),
            vmem((128, 384), F32),
            dma((12,)),
            dma((2, 4)), dma((2, 4)), dma((CHIPS,)), dma((CHIPS,)),
            dma((2, 4)), dma((2, 4)), dma((CHIPS,)), dma((CHIPS,)),
            dma((CHIPS, TP)), dma((CHIPS, TP)), dma((CHIPS,)), dma((TP,)),
            dma, dma, dma, dma,
        ],
        compiler_params=pltpu.CompilerParams(
            collective_id=0, has_side_effects=True, vmem_limit_bytes=56 << 20
        ),
        cost_estimate=pl.CostEstimate(flops=14 << 30, bytes_accessed=6 << 20, transcendentals=17 << 20),
    )(
        tract_offset,
        cache_len[0],
        pre_q[0],
        pre_k[0],
        pre_v[0],
        pre_ck[0],
        pre_cv[0],
        label,
        out_weight,
        dec_q.reshape(16, 1024),
        dec_k.reshape(16, HEAD),
        dec_v.reshape(16, HEAD),
        dec_ck.reshape(2048, HEAD),
        dec_cv.reshape(2048, HEAD),
    )
    return out[None], dec.reshape(1, 8, 2, 1024)


def solution(mesh):
    return jax.shard_map(
        shards,
        mesh=mesh,
        in_specs=(
            P("grp", "ctx", "tp"),
            P("grp", "ctx", "tp"),
            P("grp", "ctx", "tp"),
            P("grp", "ctx", "tp"),
            P("grp", "ctx", "tp"),
            P("grp"),
            P("grp", "ctx", None),
            P("grp", "ctx"),
            P("tp", "ctx"),
            P("grp", "ctx", None, "tp"),
            P("grp", "ctx", None, "tp"),
            P("grp", "ctx", None, "tp"),
            P("grp", "ctx", None, "tp"),
            P("grp", "ctx", None, "tp"),
            P("grp", "ctx"),
        ),
        out_specs=(P("grp", "tp", "ctx"), P("grp", "ctx", None, "tp")),
        check_vma=False,
    )
```

```python
import jax
import jax.numpy as jnp
from jax import lax
from jax.experimental import pallas as pl
from jax.experimental.pallas import tpu as pltpu
from jax.sharding import PartitionSpec as P

HEAD = 128
HEADS = 8
ROWS = 256
CHIPS = 8
TP = 8
NEG = -1e30
C2 = 128**-0.5 * 1.4426950408889634
F32, BF16 = jnp.float32, jnp.bfloat16
MESH = pl.DeviceIdType.MESH
NT = (((1,), (1,)), ((), ()))
NN = (((1,), (0,)), ((), ()))

CK, CV, SK, SV, LB, PACK = 0, 256, 512, 768, 1024, 1040


def dot(a, b, dims):
    return lax.dot_general(a, b, dims, preferred_element_type=F32)


def kernel(
    off_ref, len_ref, own_ref, tag_ref, q_hbm, k_hbm, v_hbm, ck_hbm, cv_hbm, w_hbm,
    dq_hbm, dk_hbm, dv_hbm, dck_hbm, dcv_hbm,
    out_ref, dec_ref,
    kv, q_s, qt, v_s, w_s, dq_s, dqs, dk_s, dv_s, dck_s, dcv_s,
    m_s, l_s, acc_s, abuf, pbuf, xb, yb, s0, s1, xb2, yb2, sbuf, obuf, dqp, hand, handin, own,
    lsem, ksend, krecv, ksibs, ksibr, asend, arecv, asibs, asibr,
    gsend, xrecv, yrecv, xrecv2, yrecv2, osend, orecv, dsend, drecv, hsend, hrecv,
):
    c = lax.axis_index("ctx")
    t = lax.axis_index("tp")
    g = lax.axis_index("grp")
    z = c // 2
    core = lax.rem(c, 2)
    right = (lax.rem(c + 2, 16), t, g)
    left = (lax.rem(c + 14, 16), t, g)
    sib = (c + 1 - 2 * core, t, g)
    other = (c, t, 1 - g)
    beside = (c, lax.rem(t + 1, TP), g)

    def chip(n):
        return lax.rem(n + CHIPS, CHIPS)

    def local(i, src, dst):
        return pltpu.make_async_copy(src, dst, lsem.at[i])

    def remote(src, dst, send, recv, device):
        return pltpu.make_async_remote_copy(
            src_ref=src, dst_ref=dst, send_sem=send, recv_sem=recv, device_id=device, device_id_type=MESH
        )

    mine = kv.at[z, core]
    ins = [
        local(0, ck_hbm, mine.at[pl.ds(CK, 256)]),
        local(1, k_hbm, mine.at[pl.ds(SK, 256)]),
        local(2, cv_hbm, v_s.at[0]),
        local(3, v_hbm, v_s.at[1]),
        local(4, dq_hbm, dq_s),
        local(5, q_hbm, q_s),
        local(6, w_hbm, w_s),
        local(7, dck_hbm, dck_s),
        local(8, dcv_hbm, dcv_s),
        local(9, dk_hbm, dk_s),
        local(10, dv_hbm, dv_s),
    ]
    for cp in ins:
        cp.start()

    barrier = pltpu.get_barrier_semaphore()
    for device in (right, left, sib, other):
        pl.semaphore_signal(barrier, inc=1, device_id=device, device_id_type=MESH)

    def greet(j, _):
        pl.semaphore_signal(barrier, inc=1, device_id=(c, lax.rem(t + 1 + j, TP), g), device_id_type=MESH)
        return 0

    lax.fori_loop(0, TP - 1, greet, 0)

    label = (own_ref[...] * 8 + tag_ref[...]).astype(F32)
    label = jnp.concatenate([label[:, :128], label[:, 128:], jnp.zeros((14, 128), F32)], axis=0)
    kv[z, core, LB : LB + 16, :] = label.astype(BF16)
    for i in range(5):
        ins[i].wait()
    for i, base in ((0, CV), (1, SV)):
        vt = v_s[i].astype(F32).T.astype(BF16)
        kv[z, core, base : base + 128, :] = vt[:, :128]
        kv[z, core, base + 128 : base + 256, :] = vt[:, 128:]
    for h in range(HEADS):
        dqs[h * 16 : (h + 1) * 16, :] = dq_s[:, h * HEAD : (h + 1) * HEAD]

    pl.semaphore_wait(barrier, 4 + TP - 1)

    class Ring:
        def __init__(self, part, send, recv, sibs, sibr):
            self.part, self.send, self.recv, self.sibs, self.sibr = part, send, recv, sibs, sibr

        def hop(self, way, n, u, k):
            part = self.part(n, core, u)
            return remote(part, part, self.send(way, k, u), self.recv(way, k, u), (right, left)[way])

        def to_sib(self, n, u):
            part = self.part(n, core, u)
            return remote(part, part, self.sibs(n, u), self.sibr(n, u), sib)

        def from_sib(self, n, u):
            part = self.part(n, 1 - core, u)
            return remote(part, part, self.sibs(n, u), self.sibr(n, u), sib)

        def begin(self):
            for u in (0, 1):
                self.hop(0, z, u, 0).start()
                self.hop(1, z, u, 0).start()
                self.to_sib(z, u).start()

        def event(self, k, u):
            before, after = chip(z - k), chip(z + k)
            self.hop(0, before, u, k - 1).wait_recv()
            self.hop(1, after, u, k - 1).wait_recv()

            @pl.when(k < 3)
            def _():
                self.hop(0, before, u, k).start()
                self.hop(1, after, u, k).start()

            @pl.when(k == 3)
            def _():
                self.hop(u, (before, after)[u], u, 3).start()

            self.to_sib(before, u).start()
            self.to_sib(after, u).start()

        def last(self, u):
            self.hop(u, chip(z + 4), u, 3).wait_recv()
            self.to_sib(chip(z + 4), u).start()

        def drain(self):
            def sent(k, _):
                for u in (0, 1):
                    self.hop(0, chip(z - k), u, k).wait_send()
                    self.hop(1, chip(z + k), u, k).wait_send()
                return 0

            lax.fori_loop(0, 3, sent, 0)
            self.hop(0, chip(z - 3), 0, 3).wait_send()
            self.hop(1, chip(z + 3), 1, 3).wait_send()

            def passed(n, _):
                for u in (0, 1):
                    self.to_sib(n, u).wait_send()
                return 0

            lax.fori_loop(0, CHIPS, passed, 0)

    far = chip(z + 4)
    kvr = Ring(
        lambda n, k, u: kv.at[n, k, pl.ds((0, SK)[u], (SK, PACK - SK)[u])],
        lambda w, k, u: ksend.at[w, k, u],
        lambda w, k, u: krecv.at[w, k, u],
        lambda n, u: ksibs.at[n, u],
        lambda n, u: ksibr.at[n, u],
    )

    def rows_ring(h):
        return Ring(
            lambda n, k, u: abuf.at[h, n, k, pl.ds(u * 64, 64)],
            lambda w, k, u: asend.at[2 * h + w, k, u],
            lambda w, k, u: arecv.at[2 * h + w, k, u],
            lambda n, u: asibs.at[2 * h + u, n],
            lambda n, u: asibr.at[2 * h + u, n],
        )

    atr = [rows_ring(0), rows_ring(1)]
    dq_copy = remote(dqs, dqp, dsend, drecv, other)
    kvr.begin()
    dq_copy.start()

    m_s[...] = jnp.full_like(m_s, NEG)
    l_s[...] = jnp.zeros_like(l_s)
    acc_s[...] = jnp.zeros_like(acc_s)
    for state in (hand, own):
        state[:, 0:128] = jnp.zeros((128, 128), F32)
        state[:, 128:256] = jnp.full((128, 128), NEG, F32)
        state[:, 256:384] = jnp.zeros((128, 128), F32)
    ins[5].wait()
    for i in range(HEADS):
        rows = slice(i // 4 * 128, i // 4 * 128 + 128)
        for j in (0, 1):
            head = i % 4 * 2 + j
            qt[i, j * 128 : (j + 1) * 128, :] = q_s[rows, head * HEAD : (head + 1) * HEAD]

    def values_of(n, k, base):
        return jnp.concatenate([kv[n, k, base : base + 128, :], kv[n, k, base + 128 : base + 256, :]], axis=1)

    key_row = lax.broadcasted_iota(jnp.int32, (256, 256), 0)
    query_row = lax.rem(lax.broadcasted_iota(jnp.int32, (256, 256), 1), 128)

    def attend(half, blocks):
        tiles = range(4 * half, 4 * half + 4)

        def scores(i):
            return [dot(kv[n, k, kb : kb + 256, :], qt[i], NT) for n, k, kb, _, _ in blocks]

        following = scores(tiles[0])
        for i in tiles:
            ss = following
            if i != tiles[-1]:
                following = scores(i + 1)
            ss = [s if b[4] is None else jnp.where(b[4], s, -jnp.inf) for s, b in zip(ss, blocks)]
            top = ss[0]
            for s in ss[1:]:
                top = jnp.maximum(top, s)
            before = m_s[i]
            now = jnp.maximum(before, jnp.max(top, axis=0, keepdims=True))
            rescale = jnp.exp2((before - now) * C2)
            shift = now * C2
            total = None
            acc = acc_s[i] * rescale
            for s, (n, k, _, vb, _) in zip(ss, blocks):
                p = jnp.exp2(s * C2 - shift)
                total = p if total is None else total + p
                acc = acc + dot(values_of(n, k, vb), p.astype(BF16), NN)
            m_s[i] = now
            l_s[i] = l_s[i] * rescale + jnp.sum(total, axis=0, keepdims=True)
            acc_s[i] = acc

    def prefix(n):
        live = off_ref[0]
        return [(n, k, CK, CV, key_row < live - (2 * n + k) * 256) for k in (0, 1)]

    def stretch(n):
        return [(n, k, SK, SV, None) for k in (0, 1)]

    def diagonal(half):
        return [(z, k, SK, SV, key_row + (k - core) * 256 <= query_row + half * 128) for k in (0, 1)]

    def visible(half, k):
        @pl.when((z >= k) & (z + k >= CHIPS))
        def _():
            attend(half, stretch(z - k) + stretch(z + k - CHIPS))

        @pl.when((z >= k) & (z + k < CHIPS))
        def _():
            attend(half, stretch(z - k))

    def farthest(half):
        @pl.when(z >= 4)
        def _():
            attend(half, prefix(far) + stretch(z - 4))

        @pl.when(z < 4)
        def _():
            attend(half, prefix(far))

    def settle(half):
        for p in range(4):
            i = 4 * half + p
            rows = (acc_s[i] / l_s[i]).T.astype(BF16)
            for j in (0, 1):
                head = 2 * p + j
                abuf[half, z, core, :, head * HEAD : (head + 1) * HEAD] = rows[j * 128 : (j + 1) * 128]

    y, x = t // 2, lax.rem(t, 2)
    across = (c, t + 1 - 2 * x, g)

    def along(j):
        return (c, lax.rem(y + j, 4) * 2 + x, g)

    def rows_at(i, n):
        return pl.ds(pl.multiple_of(i * n, n), n)

    def stand_in(buf, send, recv):
        return remote(buf, buf, send, recv, beside)

    def project(h, n):
        for u in (0, 1):
            atr[h].from_sib(n, u).wait_recv()
        rows = dot(abuf[h, n].reshape(256, 1024), w_s[...], NN).astype(BF16)
        pbuf[h, n, 0] = rows[:, :256]
        pbuf[h, n, 1] = rows[:, 256:]
        remote(pbuf.at[h, n, 0, rows_at(1 - x, 128)], xb.at[h, n], gsend.at[0], xrecv.at[h, n], across).start()
        for j in (1, 2, 3):
            to = lax.rem(y + j, 4)
            remote(
                pbuf.at[h, n, 1, rows_at(to, 64)], yb.at[h, n, j - 1], gsend.at[1], yrecv.at[h, n], along(j)
            ).start()

    def middle(h, n):
        stand_in(xb.at[h, n], gsend.at[0], xrecv.at[h, n]).wait_recv()
        total = pbuf[h, n, 0, rows_at(x, 128), :].astype(F32) + xb[h, n].astype(F32)
        s0[h, n] = total.astype(BF16)
        for j in (1, 2, 3):
            to = lax.rem(y + j, 4)
            remote(
                s0.at[h, n, rows_at(to, 32)], yb2.at[h, n, j - 1], gsend.at[2], yrecv2.at[h, n], along(j)
            ).start()
        stand_in(yb.at[h, n], gsend.at[1], yrecv.at[h, n]).wait_recv()
        total = pbuf[h, n, 1, rows_at(y, 64), :].astype(F32)
        for j in range(3):
            total = total + yb[h, n, j].astype(F32)
        s1[h, n] = total.astype(BF16)
        remote(s1.at[h, n, rows_at(1 - x, 32)], xb2.at[h, n], gsend.at[3], xrecv2.at[h, n], across).start()

    def collect(h, n):
        stand_in(yb2.at[h, n], gsend.at[2], yrecv2.at[h, n]).wait_recv()
        first = s0[h, n, rows_at(y, 32), :].astype(F32)
        for j in range(3):
            first = first + yb2[h, n, j].astype(F32)
        stand_in(xb2.at[h, n], gsend.at[3], xrecv2.at[h, n]).wait_recv()
        second = s1[h, n, rows_at(x, 32), :].astype(F32) + xb2[h, n].astype(F32)

        @pl.when(n == t)
        def _():
            obuf[h, t, 0] = first.astype(BF16)
            obuf[h, t, 1] = second.astype(BF16)

        @pl.when(n != t)
        def _():
            sbuf[h, n, 0] = first.astype(BF16)
            sbuf[h, n, 1] = second.astype(BF16)
            remote(sbuf.at[h, n], obuf.at[h, t], osend.at[h], orecv.at[h], (c, n, g)).start()

    row_id = lax.broadcasted_iota(jnp.int32, (128, 256), 0)
    col_id = lax.broadcasted_iota(jnp.int32, (128, 256), 1)
    request = lax.rem(row_id, 16) // 2

    def fold(state, parts):
        acc, m, l = state[:, 0:128], state[:, 128:129], state[:, 256:257]
        now = m
        for s, _ in parts:
            now = jnp.maximum(now, jnp.max(s, axis=1, keepdims=True))
        rescale = jnp.exp2((m - now) * C2)
        l = l * rescale
        acc = acc * rescale
        for s, weigh in parts:
            p = jnp.exp2((s - now) * C2)
            l = l + jnp.sum(p, axis=1, keepdims=True)
            acc = acc + weigh(p.astype(BF16))
        state[:, 0:128] = acc
        state[:, 128:256] = jnp.broadcast_to(now, (128, 128))
        state[:, 256:384] = jnp.broadcast_to(l, (128, 128))

    def hand_over(first, last):
        wanted = (request + c * 8).astype(F32)

        def one(n, _):
            parts = []
            for k in (0, 1):
                labels = kv[n, k, LB : LB + 16, :].astype(F32)
                label = jnp.concatenate([labels[0:1], labels[1:2]], axis=1)
                s = dot(dqp[...], kv[n, k, SK : SK + 256, :], NT)
                s = jnp.where(label == wanted, s, -jnp.inf)
                parts.append((s, lambda p, k=k: dot(p, values_of(n, k, SV), NT)))
            fold(hand, parts)
            return 0

        lax.fori_loop(first, last, one, 0)

    def cached(first, last):
        def one(i, _):
            parts = []
            for k in (0, 1):
                r = 2 * i + k
                rows = pl.ds(pl.multiple_of(r * 256, 256), 256)
                s = dot(dqs[...], dck_s[rows, :], NT)
                s = jnp.where((request == r) & (col_id < len_ref[r]), s, -jnp.inf)
                parts.append((s, lambda p, rows=rows: dot(p, dcv_s[rows, :], NN)))
            fold(own, parts)
            return 0

        lax.fori_loop(first, last, one, 0)

    def fresh():
        rows16 = lax.broadcasted_iota(jnp.int32, (128, 16), 0)
        cols16 = lax.broadcasted_iota(jnp.int32, (128, 16), 1)
        seen = (lax.rem(rows16, 16) // 2 == cols16 // 2) & (lax.rem(cols16, 2) <= lax.rem(rows16, 2))
        s = jnp.where(seen, dot(dqs[...], dk_s[...], NT), -jnp.inf)
        fold(own, [(s, lambda p: dot(p, dv_s[...], NN))])

    hand_copy = remote(hand, handin, hsend, hrecv, other)

    for u in (0, 1):
        kvr.from_sib(z, u).wait_recv()
    attend(0, prefix(z) + diagonal(0))

    def kv_step(k, _):
        before, after = chip(z - k), chip(z + k)
        kvr.event(k, 0)

        @pl.when(k > 1)
        def _():
            kvr.from_sib(chip(z - k + 1), 1).wait_recv()
            kvr.from_sib(chip(z + k - 1), 1).wait_recv()
            visible(0, k - 1)

        kvr.event(k, 1)
        kvr.from_sib(before, 0).wait_recv()
        kvr.from_sib(after, 0).wait_recv()
        attend(0, prefix(before) + prefix(after))
        return 0

    lax.fori_loop(1, 4, kv_step, 0)
    kvr.last(0)
    kvr.from_sib(chip(z - 3), 1).wait_recv()
    kvr.from_sib(chip(z + 3), 1).wait_recv()
    visible(0, 3)
    kvr.last(1)
    kvr.from_sib(far, 0).wait_recv()
    kvr.from_sib(far, 1).wait_recv()
    farthest(0)
    settle(0)

    atr[0].begin()
    attend(1, prefix(z) + diagonal(1))
    ins[6].wait()
    project(0, z)

    def first_step(k, _):
        before, after = chip(z - k), chip(z + k)
        atr[0].event(k, 0)
        visible(1, k)
        atr[0].event(k, 1)
        attend(1, prefix(before) + prefix(after))
        project(0, before)
        project(0, after)

        @pl.when(k == 1)
        def _():
            middle(0, z)

        @pl.when(k == 2)
        def _():
            middle(0, chip(z - 1))
            middle(0, chip(z + 1))
            collect(0, z)

        @pl.when(k == 3)
        def _():
            middle(0, chip(z - 2))
            middle(0, chip(z + 2))
            collect(0, chip(z - 1))
            collect(0, chip(z + 1))

        return 0

    lax.fori_loop(1, 4, first_step, 0)
    farthest(1)
    settle(1)
    atr[1].begin()
    atr[0].last(0)
    atr[0].last(1)
    middle(0, chip(z - 3))
    middle(0, chip(z + 3))
    project(0, far)
    collect(0, chip(z - 2))
    collect(0, chip(z + 2))
    project(1, z)
    dq_copy.wait_recv()
    for i in range(7, 11):
        ins[i].wait()

    def second_step(k, _):
        before, after = chip(z - k), chip(z + k)
        atr[1].event(k, 0)

        @pl.when(k == 1)
        def _():
            hand_over(0, 4)

        @pl.when(k == 2)
        def _():
            cached(0, 2)

        atr[1].event(k, 1)
        project(1, before)
        project(1, after)

        @pl.when(k == 1)
        def _():
            middle(0, far)
            middle(1, z)
            collect(0, chip(z - 3))
            collect(0, chip(z + 3))
            hand_over(4, 8)
            hand_copy.start()

        @pl.when(k == 2)
        def _():
            middle(1, chip(z - 1))
            middle(1, chip(z + 1))
            collect(0, far)
            collect(1, z)
            cached(2, 4)
            fresh()

        @pl.when(k == 3)
        def _():
            middle(1, chip(z - 2))
            middle(1, chip(z + 2))
            collect(1, chip(z - 1))
            collect(1, chip(z + 1))

        return 0

    lax.fori_loop(1, 4, second_step, 0)
    atr[1].last(0)
    atr[1].last(1)
    middle(1, chip(z - 3))
    middle(1, chip(z + 3))
    project(1, far)
    collect(1, chip(z - 2))
    collect(1, chip(z + 2))

    hand_copy.wait_recv()
    m, l = own[:, 128:129], own[:, 256:257]
    m_h, l_h = handin[:, 128:129], handin[:, 256:257]
    top = jnp.maximum(m, m_h)
    a, b = jnp.exp2((m - top) * C2), jnp.exp2((m_h - top) * C2)
    result = (own[:, 0:128] * a + handin[:, 0:128] * b) / (l * a + l_h * b)
    for h in range(HEADS):
        dec_ref[:, h * HEAD : (h + 1) * HEAD] = result[h * 16 : (h + 1) * 16].astype(BF16)

    collect(1, chip(z - 3))
    collect(1, chip(z + 3))
    middle(1, far)
    collect(1, far)

    def sums(h):
        seven = obuf.at[h, pl.ds(0, TP - 1)]
        return remote(seven, seven, osend.at[h], orecv.at[h], beside)

    for h in (0, 1):
        sums(h).wait_recv()
        for j in range(TP):
            for half, row in ((0, j % 2 * 128 + j // 2 * 32), (1, j * 32)):
                first = row // 128 * 256 + h * 128 + row % 128
                out_ref[first : first + 32, half * 256 : (half + 1) * 256] = obuf[h, j, half]

    dq_copy.wait_send()
    hand_copy.wait_send()
    kvr.drain()
    for h in (0, 1):
        atr[h].drain()
        sums(h).wait_send()
    for i, buf in enumerate((xb, yb, yb2, xb2)):
        stand_in(buf, gsend.at[i], gsend.at[i]).wait_send()


def shards(
    pre_q, pre_k, pre_v, pre_ck, pre_cv, tract_offset, owner, tag, out_weight,
    dec_q, dec_k, dec_v, dec_ck, dec_cv, cache_len,
):
    vmem, dma = pltpu.VMEM, pltpu.SemaphoreType.DMA
    anywhere = pl.BlockSpec(memory_space=pl.ANY)
    smem = pl.BlockSpec(memory_space=pltpu.SMEM)
    whole = pl.BlockSpec(memory_space=pltpu.VMEM)
    out, dec = pl.pallas_call(
        kernel,
        out_shape=(jax.ShapeDtypeStruct((512, 512), BF16), jax.ShapeDtypeStruct((16, 1024), BF16)),
        in_specs=[smem, smem, whole, whole] + [anywhere] * 11,
        out_specs=(whole, whole),
        scratch_shapes=[
            vmem((CHIPS, 2, PACK, HEAD), BF16),
            vmem((ROWS, 1024), BF16),
            vmem((HEADS, 256, HEAD), BF16),
            vmem((2, ROWS, HEAD), BF16),
            vmem((1024, 512), BF16),
            vmem((16, 1024), BF16),
            vmem((128, HEAD), BF16),
            vmem((16, HEAD), BF16),
            vmem((16, HEAD), BF16),
            vmem((2048, HEAD), BF16),
            vmem((2048, HEAD), BF16),
            vmem((HEADS, 1, ROWS), F32),
            vmem((HEADS, 1, ROWS), F32),
            vmem((HEADS, HEAD, ROWS), F32),
            vmem((2, CHIPS, 2, 128, 1024), BF16),
            vmem((2, CHIPS, 2, 256, 256), BF16),
            vmem((2, CHIPS, 128, 256), BF16),
            vmem((2, CHIPS, 3, 64, 256), BF16),
            vmem((2, CHIPS, 128, 256), BF16),
            vmem((2, CHIPS, 64, 256), BF16),
            vmem((2, CHIPS, 32, 256), BF16),
            vmem((2, CHIPS, 3, 32, 256), BF16),
            vmem((2, CHIPS, 2, 32, 256), BF16),
            vmem((2, TP, 2, 32, 256), BF16),
            vmem((128, HEAD), BF16),
            vmem((128, 384), F32),
            vmem((128, 384), F32),
            vmem((128, 384), F32),
            dma((11,)),
            dma((2, 4, 2)), dma((2, 4, 2)), dma((CHIPS, 2)), dma((CHIPS, 2)),
            dma((4, 4, 2)), dma((4, 4, 2)), dma((4, CHIPS)), dma((4, CHIPS)),
            dma((4,)), dma((2, CHIPS)), dma((2, CHIPS)), dma((2, CHIPS)), dma((2, CHIPS)), dma((2,)), dma((2,)),
            dma, dma, dma, dma,
        ],
        compiler_params=pltpu.CompilerParams(
            collective_id=0, has_side_effects=True, vmem_limit_bytes=56 << 20
        ),
        cost_estimate=pl.CostEstimate(flops=14 << 30, bytes_accessed=6 << 20, transcendentals=17 << 20),
    )(
        tract_offset,
        cache_len[0],
        owner.reshape(1, ROWS),
        tag,
        pre_q[0],
        pre_k[0],
        pre_v[0],
        pre_ck[0],
        pre_cv[0],
        out_weight,
        dec_q.reshape(16, 1024),
        dec_k.reshape(16, HEAD),
        dec_v.reshape(16, HEAD),
        dec_ck.reshape(2048, HEAD),
        dec_cv.reshape(2048, HEAD),
    )
    return out[None], dec.reshape(1, 8, 2, 1024)


def solution(mesh):
    return jax.shard_map(
        shards,
        mesh=mesh,
        in_specs=(
            P("grp", "ctx", "tp"),
            P("grp", "ctx", "tp"),
            P("grp", "ctx", "tp"),
            P("grp", "ctx", "tp"),
            P("grp", "ctx", "tp"),
            P("grp"),
            P("grp", "ctx", None),
            P("grp", "ctx"),
            P("tp", "ctx"),
            P("grp", "ctx", None, "tp"),
            P("grp", "ctx", None, "tp"),
            P("grp", "ctx", None, "tp"),
            P("grp", "ctx", None, "tp"),
            P("grp", "ctx", None, "tp"),
            P("grp", "ctx"),
        ),
        out_specs=(P("grp", "tp", "ctx"), P("grp", "ctx", None, "tp")),
        check_vma=False,
    )
```

```python
import jax
import jax.numpy as jnp
from jax import lax
from jax.experimental import pallas as pl
from jax.experimental.pallas import tpu as pltpu
from jax.sharding import PartitionSpec as P

HEAD = 128
HEADS = 8
ROWS = 256
CHIPS = 8
TP = 8
NEG = -1e30
C2 = 128**-0.5 * 1.4426950408889634
F32, BF16 = jnp.float32, jnp.bfloat16
MESH = pl.DeviceIdType.MESH
NT = (((1,), (1,)), ((), ()))
NN = (((1,), (0,)), ((), ()))

CK, CV, SK, SV, LB, PACK = 0, 256, 512, 768, 1024, 1040


def dot(a, b, dims):
    return lax.dot_general(a, b, dims, preferred_element_type=F32)


def kernel(
    off_ref, len_ref, own_ref, tag_ref, q_hbm, k_hbm, v_hbm, ck_hbm, cv_hbm, w_hbm,
    dq_hbm, dk_hbm, dv_hbm, dck_hbm, dcv_hbm,
    out_ref, dec_ref,
    kv, q_s, qt, v_s, w_s, dq_s, dqs, dk_s, dv_s, dck_s, dcv_s,
    m_s, l_s, acc_s, abuf, pbuf, xb, yb, s0, s1, xb2, yb2, rb, sbuf, obuf, dqp, hand, handin, own,
    lsem, ksend, krecv, ksibs, ksibr, asend, arecv, asibs, asibr,
    gsend, xrecv, yrecv, xrecv2, yrecv2, rrecv, osend, orecv, dsend, drecv, hsend, hrecv,
):
    c = lax.axis_index("ctx")
    t = lax.axis_index("tp")
    g = lax.axis_index("grp")
    z = c // 2
    core = lax.rem(c, 2)
    right = (lax.rem(c + 2, 16), t, g)
    left = (lax.rem(c + 14, 16), t, g)
    sib = (c + 1 - 2 * core, t, g)
    other = (c, t, 1 - g)
    beside = (c, lax.rem(t + 1, TP), g)

    def chip(n):
        return lax.rem(n + CHIPS, CHIPS)

    def local(i, src, dst):
        return pltpu.make_async_copy(src, dst, lsem.at[i])

    def remote(src, dst, send, recv, device):
        return pltpu.make_async_remote_copy(
            src_ref=src, dst_ref=dst, send_sem=send, recv_sem=recv, device_id=device, device_id_type=MESH
        )

    mine = kv.at[z, core]
    ins = [
        local(0, ck_hbm, mine.at[pl.ds(CK, 256)]),
        local(1, k_hbm, mine.at[pl.ds(SK, 256)]),
        local(2, cv_hbm, v_s.at[0]),
        local(3, v_hbm, v_s.at[1]),
        local(4, dq_hbm, dq_s),
        local(5, q_hbm, q_s),
        local(6, w_hbm, w_s),
        local(7, dck_hbm, dck_s),
        local(8, dcv_hbm, dcv_s),
        local(9, dk_hbm, dk_s),
        local(10, dv_hbm, dv_s),
    ]
    for cp in ins:
        cp.start()

    barrier = pltpu.get_barrier_semaphore()
    for device in (right, left, sib, other):
        pl.semaphore_signal(barrier, inc=1, device_id=device, device_id_type=MESH)

    def greet(j, _):
        pl.semaphore_signal(barrier, inc=1, device_id=(c, lax.rem(t + 1 + j, TP), g), device_id_type=MESH)
        return 0

    lax.fori_loop(0, TP - 1, greet, 0)

    label = (own_ref[...] * 8 + tag_ref[...]).astype(F32)
    label = jnp.concatenate([label[:, :128], label[:, 128:], jnp.zeros((14, 128), F32)], axis=0)
    kv[z, core, LB : LB + 16, :] = label.astype(BF16)
    for i in range(5):
        ins[i].wait()
    for i, base in ((0, CV), (1, SV)):
        vt = v_s[i].astype(F32).T.astype(BF16)
        kv[z, core, base : base + 128, :] = vt[:, :128]
        kv[z, core, base + 128 : base + 256, :] = vt[:, 128:]
    for h in range(HEADS):
        dqs[h * 16 : (h + 1) * 16, :] = dq_s[:, :, h * HEAD : (h + 1) * HEAD].astype(F32).reshape(16, HEAD).astype(BF16)

    pl.semaphore_wait(barrier, 4 + TP - 1)

    class Ring:
        def __init__(self, part, pair, send, recv, sibs, sibr):
            self.part, self.pair, self.send, self.recv, self.sibs, self.sibr = part, pair, send, recv, sibs, sibr

        def hop(self, way, n, u, k):
            part = self.part(n, core, u)
            return remote(part, part, self.send, self.recv(way, k, u), (right, left)[way])

        def to_sib(self, n, v):
            pair = self.pair(n, core, v)
            return remote(pair, pair, self.sibs, self.sibr(n, v), sib)

        def from_sib(self, n, v):
            pair = self.pair(n, 1 - core, v)
            return remote(pair, pair, self.sibs, self.sibr(n, v), sib)

        def begin(self, u):
            self.hop(0, z, u, 0).start()
            self.hop(1, z, u, 0).start()
            if u % 2:
                self.to_sib(z, u // 2).start()

        def event(self, k, v):
            before, after = chip(z - k), chip(z + k)
            for u in (2 * v, 2 * v + 1):
                self.hop(0, before, u, k - 1).wait_recv()

                @pl.when(k < 3)
                def _():
                    self.hop(0, before, u, k).start()

                self.hop(1, after, u, k - 1).wait_recv()

                @pl.when(k < 3)
                def _():
                    self.hop(1, after, u, k).start()

                @pl.when(k == 3)
                def _():
                    self.hop(v, (before, after)[v], u, 3).start()

            self.to_sib(before, v).start()
            self.to_sib(after, v).start()

        def last(self, v):
            for u in (2 * v, 2 * v + 1):
                self.hop(v, chip(z + 4), u, 3).wait_recv()
            self.to_sib(chip(z + 4), v).start()

        def drain(self, blocks):
            seven, eight = blocks(pl.ds(0, 7)), blocks(pl.ds(0, 8))
            remote(seven, seven, self.send, self.recv(0, 0, 0), right).wait_send()
            remote(eight, eight, self.sibs, self.sibr(0, 0), sib).wait_send()

    far = chip(z + 4)
    kvr = Ring(
        lambda n, k, u: kv.at[n, k, pl.ds(256 * u, (256, 256, 256, PACK - SV)[u])],
        lambda n, k, v: kv.at[n, k, pl.ds((0, SK)[v], (SK, PACK - SK)[v])],
        ksend,
        lambda w, k, u: krecv.at[w, k, u],
        ksibs,
        lambda n, u: ksibr.at[n, u],
    )

    def rows_ring(h):
        return Ring(
            lambda n, k, u: abuf.at[h, n, k, u],
            lambda n, k, v: abuf.at[h, n, k, pl.ds(2 * v, 2)],
            asend.at[h],
            lambda w, k, u: arecv.at[2 * h + w, k, u],
            asibs.at[h],
            lambda n, v: asibr.at[2 * h + v, n],
        )

    atr = [rows_ring(0), rows_ring(1)]
    dq_copy = remote(dqs, dqp, dsend, drecv, other)
    for u in range(4):
        kvr.begin(u)
    dq_copy.start()

    m_s[...] = jnp.full_like(m_s, NEG)
    l_s[...] = jnp.zeros_like(l_s)
    acc_s[...] = jnp.zeros_like(acc_s)
    for state in (hand, own):
        state[:, 0:128] = jnp.zeros((128, 128), F32)
        state[:, 128:256] = jnp.full((128, 128), NEG, F32)
        state[:, 256:384] = jnp.zeros((128, 128), F32)
    ins[5].wait()
    for i in range(HEADS):
        rows = slice(i // 4 * 128, i // 4 * 128 + 128)
        for j in (0, 1):
            head = i % 4 * 2 + j
            qt[i, j * 128 : (j + 1) * 128, :] = q_s[rows, head * HEAD : (head + 1) * HEAD]

    def values_of(n, k, base):
        return jnp.concatenate([kv[n, k, base : base + 128, :], kv[n, k, base + 128 : base + 256, :]], axis=1)

    key_row = lax.broadcasted_iota(jnp.int32, (256, 256), 0)
    query_row = lax.rem(lax.broadcasted_iota(jnp.int32, (256, 256), 1), 128)

    def attend(tiles, blocks):
        def scores(i):
            ss = [dot(kv[n, k, kb : kb + 256, :], qt[i], NT) for n, k, kb, _, _ in blocks]
            return [s if b[4] is None else jnp.where(b[4](i // 4), s, -jnp.inf) for s, b in zip(ss, blocks)]

        following = scores(tiles[0])
        for i in tiles:
            ss = following
            if i != tiles[-1]:
                following = scores(i + 1)
            top = ss[0]
            for s in ss[1:]:
                top = jnp.maximum(top, s)
            before = m_s[i]
            now = jnp.maximum(before, jnp.max(top, axis=0, keepdims=True))
            rescale = jnp.exp2((before - now) * C2)
            shift = now * C2
            total = None
            acc = acc_s[i] * rescale
            for s, (n, k, _, vb, _) in zip(ss, blocks):
                p = jnp.exp2(s * C2 - shift)
                total = p if total is None else total + p
                acc = acc + dot(values_of(n, k, vb), p.astype(BF16), NN)
            m_s[i] = now
            l_s[i] = l_s[i] * rescale + jnp.sum(total, axis=0, keepdims=True)
            acc_s[i] = acc

    def prefix(n):
        live = off_ref[0]
        return [(n, k, CK, CV, lambda half, k=k: key_row < live - (2 * n + k) * 256) for k in (0, 1)]

    def stretch(n):
        return [(n, k, SK, SV, None) for k in (0, 1)]

    def diagonal():
        def until(k):
            return lambda half: key_row + (k - core) * 256 <= query_row + half * 128

        return [(z, k, SK, SV, until(k)) for k in (0, 1)]

    def visible(tiles, k):
        @pl.when((z >= k) & (z + k >= CHIPS))
        def _():
            attend(tiles, stretch(z - k) + stretch(z + k - CHIPS))

        @pl.when((z >= k) & (z + k < CHIPS))
        def _():
            attend(tiles, stretch(z - k))

    def farthest(tiles):
        @pl.when(z >= 4)
        def _():
            attend(tiles, prefix(far) + stretch(z - 4))

        @pl.when(z < 4)
        def _():
            attend(tiles, prefix(far))

    def settle(half, u):
        for p in (0, 1):
            i = 4 * half + 2 * u + p
            rows = (acc_s[i] / l_s[i]).T.astype(BF16)
            for j in (0, 1):
                abuf[half, z, core, 2 * u + p, :, j * HEAD : (j + 1) * HEAD] = rows[j * 128 : (j + 1) * 128]
            atr[half].begin(2 * u + p)

    y, x = t // 2, lax.rem(t, 2)
    across = (c, t + 1 - 2 * x, g)

    def along(j):
        return (c, lax.rem(y + j, 4) * 2 + x, g)

    def stand_in(buf, send, recv):
        return remote(buf, buf, send, recv, beside)

    def multiply(h, n):
        for u in (0, 1):
            atr[h].from_sib(n, u).wait_recv()
        rows = jnp.concatenate([abuf[h, n, :, u].reshape(256, 256) for u in range(4)], axis=1)
        rows = dot(rows, w_s[...], NN).astype(BF16)
        pbuf[h, n, 0] = rows[:, :256].reshape(4, 2, 32, 256)
        pbuf[h, n, 1] = rows[:, 256:].reshape(4, 2, 32, 256)

    def spread(h, n):
        remote(pbuf.at[h, n, 0, :, 1 - x], xb.at[CHIPS * h + n], gsend.at[0], xrecv.at[h, n], across).start()
        for j in (1, 2, 3):
            to = lax.rem(y + j, 4)
            remote(
                pbuf.at[h, n, 1, to], yb.at[CHIPS * h + n, j - 1], gsend.at[1], yrecv.at[h, n], along(j)
            ).start()

    def project(h, n):
        multiply(h, n)
        spread(h, n)

    def middle(h, n):
        stand_in(xb.at[CHIPS * h + n], gsend.at[0], xrecv.at[h, n]).wait_recv()
        total = pbuf[h, n, 0, :, x].astype(F32) + xb[CHIPS * h + n].astype(F32)
        s0[h, n] = total.astype(BF16)
        for j in (1, 2, 3):
            to = lax.rem(y + j, 4)
            remote(
                s0.at[h, n, to], yb2.at[CHIPS * h + n, j - 1], gsend.at[2], yrecv2.at[h, n], along(j)
            ).start()
        stand_in(yb.at[CHIPS * h + n], gsend.at[1], yrecv.at[h, n]).wait_recv()
        total = pbuf[h, n, 1, y].astype(F32)
        for j in range(3):
            total = total + yb[CHIPS * h + n, j].astype(F32)
        s1[h, n] = total.astype(BF16)
        remote(s1.at[h, n, 1 - x], xb2.at[CHIPS * h + n], gsend.at[3], xrecv2.at[h, n], across).start()

    def collect(h, n):
        stand_in(yb2.at[CHIPS * h + n], gsend.at[2], yrecv2.at[h, n]).wait_recv()
        first = s0[h, n, y].astype(F32)
        for j in range(3):
            first = first + yb2[CHIPS * h + n, j].astype(F32)
        stand_in(xb2.at[CHIPS * h + n], gsend.at[3], xrecv2.at[h, n]).wait_recv()
        second = s1[h, n, x].astype(F32) + xb2[CHIPS * h + n].astype(F32)

        hand_in(h, n, first, second)

    def hand_in(h, n, first, second):
        @pl.when(n == t)
        def _():
            obuf[h, t, 0] = first.astype(BF16)
            obuf[h, t, 1] = second.astype(BF16)

        @pl.when(n != t)
        def _():
            sbuf[h, n, 0] = first.astype(BF16)
            sbuf[h, n, 1] = second.astype(BF16)
            remote(sbuf.at[h, n], obuf.at[h, t], osend.at[h], orecv.at[h], (c, n, g)).start()

    def spread_last():
        def send(j, _):
            to = lax.rem(t + 1 + j, TP)
            remote(
                pbuf.at[1, far, :, to // 2, lax.rem(to, 2)], rb.at[j], gsend.at[4], rrecv, (c, to, g)
            ).start()
            return 0

        lax.fori_loop(0, TP - 1, send, 0)

    def collect_last():
        stand_in(rb, gsend.at[4], rrecv).wait_recv()
        total = pbuf[1, far, :, y, x].astype(F32)
        for j in range(TP - 1):
            total = total + rb[j].astype(F32)
        hand_in(1, far, total[0], total[1])

    row_id = lax.broadcasted_iota(jnp.int32, (128, 256), 0)
    col_id = lax.broadcasted_iota(jnp.int32, (128, 256), 1)
    request = lax.rem(row_id, 16) // 2

    def fold(state, parts):
        acc, m, l = state[:, 0:128], state[:, 128:129], state[:, 256:257]
        now = m
        for s, _ in parts:
            now = jnp.maximum(now, jnp.max(s, axis=1, keepdims=True))
        rescale = jnp.exp2((m - now) * C2)
        l = l * rescale
        acc = acc * rescale
        for s, weigh in parts:
            p = jnp.exp2((s - now) * C2)
            l = l + jnp.sum(p, axis=1, keepdims=True)
            acc = acc + weigh(p.astype(BF16))
        state[:, 0:128] = acc
        state[:, 128:256] = jnp.broadcast_to(now, (128, 128))
        state[:, 256:384] = jnp.broadcast_to(l, (128, 128))

    def hand_over(first, last):
        wanted = (request + c * 8).astype(F32)

        def one(n, _):
            parts = []
            for k in (0, 1):
                labels = kv[n, k, LB : LB + 16, :].astype(F32)
                label = jnp.concatenate([labels[0:1], labels[1:2]], axis=1)
                s = dot(dqp[...], kv[n, k, SK : SK + 256, :], NT)
                s = jnp.where(label == wanted, s, -jnp.inf)
                parts.append((s, lambda p, k=k: dot(p, values_of(n, k, SV), NT)))
            fold(hand, parts)
            return 0

        lax.fori_loop(first, last, one, 0)

    def cached(first, last):
        def one(i, _):
            parts = []
            for k in (0, 1):
                r = 2 * i + k
                rows = pl.ds(pl.multiple_of(r * 256, 256), 256)
                s = dot(dqs[...], dck_s[rows, :], NT)
                s = jnp.where((request == r) & (col_id < len_ref[r]), s, -jnp.inf)
                parts.append((s, lambda p, rows=rows: dot(p, dcv_s[rows, :], NN)))
            fold(own, parts)
            return 0

        lax.fori_loop(first, last, one, 0)

    def fresh():
        rows16 = lax.broadcasted_iota(jnp.int32, (128, 16), 0)
        cols16 = lax.broadcasted_iota(jnp.int32, (128, 16), 1)
        seen = (lax.rem(rows16, 16) // 2 == cols16 // 2) & (lax.rem(cols16, 2) <= lax.rem(rows16, 2))
        s = jnp.where(seen, dot(dqs[...], dk_s[...], NT), -jnp.inf)
        fold(own, [(s, lambda p: dot(p, dv_s[...], NN))])

    hand_copy = remote(hand, handin, hsend, hrecv, other)

    early, late = range(0, 5), range(5, 8)
    for u in (0, 1):
        kvr.from_sib(z, u).wait_recv()
    attend(early, prefix(z) + diagonal())

    def kv_step(k, _):
        before, after = chip(z - k), chip(z + k)
        kvr.event(k, 0)

        @pl.when(k > 1)
        def _():
            kvr.from_sib(chip(z - k + 1), 1).wait_recv()
            kvr.from_sib(chip(z + k - 1), 1).wait_recv()
            visible(early, k - 1)

        kvr.event(k, 1)
        kvr.from_sib(before, 0).wait_recv()
        kvr.from_sib(after, 0).wait_recv()
        attend(early, prefix(before) + prefix(after))
        return 0

    lax.fori_loop(1, 4, kv_step, 0)
    kvr.last(0)
    kvr.from_sib(chip(z - 3), 1).wait_recv()
    kvr.from_sib(chip(z + 3), 1).wait_recv()
    visible(early, 3)
    kvr.last(1)
    kvr.from_sib(far, 0).wait_recv()
    kvr.from_sib(far, 1).wait_recv()
    farthest((0, 1))
    settle(0, 0)
    farthest((2, 3))
    settle(0, 1)

    farthest((4,))
    attend(late, prefix(z) + diagonal())
    ins[6].wait()

    def first_step(k, _):
        before, after = chip(z - k), chip(z + k)
        atr[0].event(k, 0)
        visible(late, k)

        @pl.when(k == 1)
        def _():
            project(0, z)

        @pl.when(k > 1)
        def _():
            project(0, chip(z - k + 1))

        @pl.when(k == 2)
        def _():
            middle(0, z)

        @pl.when(k == 3)
        def _():
            middle(0, chip(z - 1))
            collect(0, z)

        atr[0].event(k, 1)
        attend(late, prefix(before) + prefix(after))

        @pl.when(k > 1)
        def _():
            project(0, chip(z + k - 1))

        @pl.when(k == 3)
        def _():
            middle(0, chip(z + 1))

        return 0

    lax.fori_loop(1, 4, first_step, 0)
    farthest(late)
    settle(1, 0)
    settle(1, 1)
    atr[0].last(0)
    atr[0].last(1)
    project(0, chip(z - 3))
    project(0, chip(z + 3))
    middle(0, chip(z - 2))
    middle(0, chip(z + 2))
    project(0, far)
    project(1, z)
    dq_copy.wait_recv()
    for i in range(7, 11):
        ins[i].wait()

    def second_step(k, _):
        before, after = chip(z - k), chip(z + k)
        atr[1].event(k, 0)

        @pl.when(k == 1)
        def _():
            collect(0, chip(z - 1))
            collect(0, chip(z + 1))
            hand_over(0, 2)

        @pl.when(k == 2)
        def _():
            collect(0, chip(z - 2))
            collect(0, chip(z + 2))
            hand_over(5, 7)

        @pl.when(k == 3)
        def _():
            collect(0, chip(z - 3))
            collect(0, chip(z + 3))
            cached(0, 2)

        atr[1].event(k, 1)
        project(1, before)
        project(1, after)

        @pl.when(k == 1)
        def _():
            middle(0, chip(z - 3))
            middle(0, chip(z + 3))
            middle(0, far)
            middle(1, z)
            hand_over(2, 5)

        @pl.when(k == 2)
        def _():
            middle(1, chip(z - 1))
            middle(1, chip(z + 1))
            hand_over(7, 8)
            hand_copy.start()

        @pl.when(k == 3)
        def _():
            middle(1, chip(z - 2))
            middle(1, chip(z + 2))
            collect(0, far)
            collect(1, z)
            collect(1, chip(z - 1))
            collect(1, chip(z + 1))

        return 0

    def sums(h):
        seven = obuf.at[h, pl.ds(0, TP - 1)]
        return remote(seven, seven, osend.at[h], orecv.at[h], beside)

    def deliver(h):
        sums(h).wait_recv()
        for j in range(TP):
            first = j // 4 * 256 + h * 128 + j % 4 * 32
            for half in (0, 1):
                out_ref[first : first + 32, half * 256 : (half + 1) * 256] = obuf[h, j, half]

    lax.fori_loop(1, 4, second_step, 0)
    cached(2, 4)
    atr[1].last(0)
    atr[1].last(1)
    middle(1, chip(z - 3))
    middle(1, chip(z + 3))
    multiply(1, far)
    spread_last()
    collect(1, chip(z - 2))
    collect(1, chip(z + 2))
    fresh()

    hand_copy.wait_recv()
    m, l = own[:, 128:129], own[:, 256:257]
    m_h, l_h = handin[:, 128:129], handin[:, 256:257]
    top = jnp.maximum(m, m_h)
    a, b = jnp.exp2((m - top) * C2), jnp.exp2((m_h - top) * C2)
    result = (own[:, 0:128] * a + handin[:, 0:128] * b) / (l * a + l_h * b)
    for h in range(HEADS):
        dec_ref[:, :, h * HEAD : (h + 1) * HEAD] = result[h * 16 : (h + 1) * 16].reshape(8, 2, HEAD).astype(BF16)
    collect(1, chip(z - 3))
    collect(1, chip(z + 3))
    collect_last()

    dq_copy.wait_send()
    hand_copy.wait_send()
    kvr.drain(lambda ns: kv.at[ns, 0])
    for h in (0, 1):
        atr[h].drain(lambda ns, h=h: abuf.at[h, ns, 0])
    deliver(0)
    for i, buf in enumerate((xb, yb, yb2, xb2)):
        most = buf.at[pl.ds(0, 2 * CHIPS - 1)]
        stand_in(most, gsend.at[i], gsend.at[i]).wait_send()
    stand_in(rb, gsend.at[4], rrecv).wait_send()
    deliver(1)
    for h in (0, 1):
        sums(h).wait_send()


def shards(
    pre_q, pre_k, pre_v, pre_ck, pre_cv, tract_offset, owner, tag, out_weight,
    dec_q, dec_k, dec_v, dec_ck, dec_cv, cache_len,
):
    vmem, dma = pltpu.VMEM, pltpu.SemaphoreType.DMA
    anywhere = pl.BlockSpec(memory_space=pl.ANY)
    smem = pl.BlockSpec(memory_space=pltpu.SMEM)
    whole = pl.BlockSpec(memory_space=pltpu.VMEM)
    out, dec = pl.pallas_call(
        kernel,
        out_shape=(jax.ShapeDtypeStruct((512, 512), BF16), jax.ShapeDtypeStruct((8, 2, 1024), BF16)),
        in_specs=[smem, smem, whole, whole] + [anywhere] * 11,
        out_specs=(whole, whole),
        scratch_shapes=[
            vmem((CHIPS, 2, PACK, HEAD), BF16),
            vmem((ROWS, 1024), BF16),
            vmem((HEADS, 256, HEAD), BF16),
            vmem((2, ROWS, HEAD), BF16),
            vmem((1024, 512), BF16),
            vmem((8, 2, 1024), BF16),
            vmem((128, HEAD), BF16),
            vmem((16, HEAD), BF16),
            vmem((16, HEAD), BF16),
            vmem((2048, HEAD), BF16),
            vmem((2048, HEAD), BF16),
            vmem((HEADS, 1, ROWS), F32),
            vmem((HEADS, 1, ROWS), F32),
            vmem((HEADS, HEAD, ROWS), F32),
            vmem((2, CHIPS, 2, 4, 128, 256), BF16),
            vmem((2, CHIPS, 2, 4, 2, 32, 256), BF16),
            vmem((2 * CHIPS, 4, 32, 256), BF16),
            vmem((2 * CHIPS, 3, 2, 32, 256), BF16),
            vmem((2, CHIPS, 4, 32, 256), BF16),
            vmem((2, CHIPS, 2, 32, 256), BF16),
            vmem((2 * CHIPS, 32, 256), BF16),
            vmem((2 * CHIPS, 3, 32, 256), BF16),
            vmem((TP - 1, 2, 32, 256), BF16),
            vmem((2, CHIPS, 2, 32, 256), BF16),
            vmem((2, TP, 2, 32, 256), BF16),
            vmem((128, HEAD), BF16),
            vmem((128, 384), F32),
            vmem((128, 384), F32),
            vmem((128, 384), F32),
            dma((11,)),
            dma, dma((2, 4, 4)), dma, dma((CHIPS, 2)),
            dma((2,)), dma((4, 4, 4)), dma((2,)), dma((4, CHIPS)),
            dma((5,)), dma((2, CHIPS)), dma((2, CHIPS)), dma((2, CHIPS)), dma((2, CHIPS)), dma, dma((2,)), dma((2,)),
            dma, dma, dma, dma,
        ],
        compiler_params=pltpu.CompilerParams(
            collective_id=0, has_side_effects=True, vmem_limit_bytes=56 << 20
        ),
        cost_estimate=pl.CostEstimate(flops=14 << 30, bytes_accessed=6 << 20, transcendentals=17 << 20),
    )(
        tract_offset,
        cache_len[0],
        owner.reshape(1, ROWS),
        tag,
        pre_q[0],
        pre_k[0],
        pre_v[0],
        pre_ck[0],
        pre_cv[0],
        out_weight,
        dec_q[0],
        dec_k.reshape(16, HEAD),
        dec_v.reshape(16, HEAD),
        dec_ck.reshape(2048, HEAD),
        dec_cv.reshape(2048, HEAD),
    )
    return out[None], dec[None]


def solution(mesh):
    return jax.shard_map(
        shards,
        mesh=mesh,
        in_specs=(
            P("grp", "ctx", "tp"),
            P("grp", "ctx", "tp"),
            P("grp", "ctx", "tp"),
            P("grp", "ctx", "tp"),
            P("grp", "ctx", "tp"),
            P("grp"),
            P("grp", "ctx", None),
            P("grp", "ctx"),
            P("tp", "ctx"),
            P("grp", "ctx", None, "tp"),
            P("grp", "ctx", None, "tp"),
            P("grp", "ctx", None, "tp"),
            P("grp", "ctx", None, "tp"),
            P("grp", "ctx", None, "tp"),
            P("grp", "ctx"),
        ),
        out_specs=(P("grp", "tp", "ctx"), P("grp", "ctx", None, "tp")),
        check_vma=False,
    )
```

```python
import jax
import jax.numpy as jnp
from jax import lax
from jax.experimental import pallas as pl
from jax.experimental.pallas import tpu as pltpu
from jax.sharding import PartitionSpec as P

HEAD = 128
HEADS = 8
ROWS = 256
CHIPS = 8
TP = 8
NEG = -1e30
C2 = 128**-0.5 * 1.4426950408889634
F32, BF16 = jnp.float32, jnp.bfloat16
MESH = pl.DeviceIdType.MESH
NT = (((1,), (1,)), ((), ()))
NN = (((1,), (0,)), ((), ()))

CK, CV, SK, SV, LB, PACK = 0, 256, 512, 768, 1024, 1040


def dot(a, b, dims):
    return lax.dot_general(a, b, dims, preferred_element_type=F32)


def kernel(
    off_ref, len_ref, own_ref, tag_ref, q_hbm, k_hbm, v_hbm, ck_hbm, cv_hbm, w_hbm,
    dq_hbm, dk_hbm, dv_hbm, dck_hbm, dcv_hbm,
    out_ref, dec_ref,
    kv, q_s, qt, v_s, w_s, dq_s, dqs, dk_s, dv_s, dck_s, dcv_s,
    m_s, l_s, acc_s, abuf, pbuf, xb, yb, s0, s1, xb2, yb2, rb, sbuf, obuf, dqp, hand, handin, own,
    lsem, ksend, krecv, ksibs, ksibr, asend, arecv, asibs, asibr,
    gsend, xrecv, yrecv, xrecv2, yrecv2, rrecv, osend, orecv, dsend, drecv, hsend, hrecv,
):
    c = lax.axis_index("ctx")
    t = lax.axis_index("tp")
    g = lax.axis_index("grp")
    z = c // 2
    core = lax.rem(c, 2)
    right = (lax.rem(c + 2, 16), t, g)
    left = (lax.rem(c + 14, 16), t, g)
    sib = (c + 1 - 2 * core, t, g)
    other = (c, t, 1 - g)
    beside = (c, lax.rem(t + 1, TP), g)

    def chip(n):
        return lax.rem(n + CHIPS, CHIPS)

    def local(i, src, dst):
        return pltpu.make_async_copy(src, dst, lsem.at[i])

    def remote(src, dst, send, recv, device):
        return pltpu.make_async_remote_copy(
            src_ref=src, dst_ref=dst, send_sem=send, recv_sem=recv, device_id=device, device_id_type=MESH
        )

    mine = kv.at[z, core]
    ins = [
        local(0, ck_hbm, mine.at[pl.ds(CK, 256)]),
        local(1, k_hbm, mine.at[pl.ds(SK, 256)]),
        local(2, cv_hbm, v_s.at[0]),
        local(3, v_hbm, v_s.at[1]),
        local(4, dq_hbm, dq_s),
        local(5, q_hbm, q_s),
        local(6, w_hbm, w_s),
        local(7, dck_hbm, dck_s),
        local(8, dcv_hbm, dcv_s),
        local(9, dk_hbm, dk_s),
        local(10, dv_hbm, dv_s),
    ]
    for cp in ins:
        cp.start()

    barrier = pltpu.get_barrier_semaphore()
    for device in (right, left, sib, other):
        pl.semaphore_signal(barrier, inc=1, device_id=device, device_id_type=MESH)

    def greet(j, _):
        pl.semaphore_signal(barrier, inc=1, device_id=(c, lax.rem(t + 1 + j, TP), g), device_id_type=MESH)
        return 0

    lax.fori_loop(0, TP - 1, greet, 0)

    class Ring:
        def __init__(self, part, pair, send, recv, sibs, sibr):
            self.part, self.pair, self.send, self.recv, self.sibs, self.sibr = part, pair, send, recv, sibs, sibr

        def hop(self, way, n, u, k):
            part = self.part(n, core, u)
            return remote(part, part, self.send, self.recv(way, k, u), (right, left)[way])

        def to_sib(self, n, v):
            pair = self.pair(n, core, v)
            return remote(pair, pair, self.sibs, self.sibr(n, v), sib)

        def from_sib(self, n, v):
            pair = self.pair(n, 1 - core, v)
            return remote(pair, pair, self.sibs, self.sibr(n, v), sib)

        def begin(self, u):
            self.hop(0, z, u, 0).start()
            self.hop(1, z, u, 0).start()
            if u % 2:
                self.to_sib(z, u // 2).start()

        def event(self, k, v):
            before, after = chip(z - k), chip(z + k)
            for u in (2 * v, 2 * v + 1):
                self.hop(0, before, u, k - 1).wait_recv()

                @pl.when(k < 3)
                def _():
                    self.hop(0, before, u, k).start()

                self.hop(1, after, u, k - 1).wait_recv()

                @pl.when(k < 3)
                def _():
                    self.hop(1, after, u, k).start()

                @pl.when(k == 3)
                def _():
                    self.hop(v, (before, after)[v], u, 3).start()

            self.to_sib(before, v).start()
            self.to_sib(after, v).start()

        def last(self, v):
            for u in (2 * v, 2 * v + 1):
                self.hop(v, chip(z + 4), u, 3).wait_recv()
            self.to_sib(chip(z + 4), v).start()

        def drain(self, blocks):
            seven, eight = blocks(pl.ds(0, 7)), blocks(pl.ds(0, 8))
            remote(seven, seven, self.send, self.recv(0, 0, 0), right).wait_send()
            remote(eight, eight, self.sibs, self.sibr(0, 0), sib).wait_send()

    far = chip(z + 4)
    kvr = Ring(
        lambda n, k, u: kv.at[n, k, pl.ds(256 * u, (256, 256, 256, PACK - SV)[u])],
        lambda n, k, v: kv.at[n, k, pl.ds((0, SK)[v], (SK, PACK - SK)[v])],
        ksend,
        lambda w, k, u: krecv.at[w, k, u],
        ksibs,
        lambda n, u: ksibr.at[n, u],
    )

    def rows_ring(h):
        return Ring(
            lambda n, k, u: abuf.at[h, n, k, u],
            lambda n, k, v: abuf.at[h, n, k, pl.ds(2 * v, 2)],
            asend.at[h],
            lambda w, k, u: arecv.at[2 * h + w, k, u],
            asibs.at[h],
            lambda n, v: asibr.at[2 * h + v, n],
        )

    atr = [rows_ring(0), rows_ring(1)]
    dq_copy = remote(dqs, dqp, dsend, drecv, other)
    def transposed(i, base):
        vt = v_s[i].astype(F32).T.astype(BF16)
        kv[z, core, base : base + 128, :] = vt[:, :128]
        kv[z, core, base + 128 : base + 256, :] = vt[:, 128:]

    ins[0].wait()
    pl.semaphore_wait(barrier, 4 + TP - 1)
    kvr.begin(0)
    ins[2].wait()
    transposed(0, CV)
    kvr.begin(1)
    ins[1].wait()
    kvr.begin(2)
    label = (own_ref[...] * 8 + tag_ref[...]).astype(F32)
    label = jnp.concatenate([label[:, :128], label[:, 128:], jnp.zeros((14, 128), F32)], axis=0)
    kv[z, core, LB : LB + 16, :] = label.astype(BF16)
    ins[3].wait()
    transposed(1, SV)
    kvr.begin(3)
    ins[4].wait()
    for h in range(HEADS):
        dqs[h * 16 : (h + 1) * 16, :] = dq_s[:, :, h * HEAD : (h + 1) * HEAD].astype(F32).reshape(16, HEAD).astype(BF16)
    dq_copy.start()

    m_s[...] = jnp.full_like(m_s, NEG)
    l_s[...] = jnp.zeros_like(l_s)
    acc_s[...] = jnp.zeros_like(acc_s)
    for state in (hand, own):
        state[:, 0:128] = jnp.zeros((128, 128), F32)
        state[:, 128:256] = jnp.full((128, 128), NEG, F32)
        state[:, 256:384] = jnp.zeros((128, 128), F32)
    ins[5].wait()
    for i in range(HEADS):
        rows = slice(i // 4 * 128, i // 4 * 128 + 128)
        for j in (0, 1):
            head = i % 4 * 2 + j
            qt[i, j * 128 : (j + 1) * 128, :] = q_s[rows, head * HEAD : (head + 1) * HEAD]

    def values_of(n, k, base):
        return jnp.concatenate([kv[n, k, base : base + 128, :], kv[n, k, base + 128 : base + 256, :]], axis=1)

    key_row = lax.broadcasted_iota(jnp.int32, (256, 256), 0)
    query_row = lax.rem(lax.broadcasted_iota(jnp.int32, (256, 256), 1), 128)

    def attend(tiles, blocks):
        def scores(i):
            ss = [dot(kv[n, k, kb : kb + 256, :], qt[i], NT) for n, k, kb, _, _ in blocks]
            return [s if b[4] is None else jnp.where(b[4](i // 4), s, -jnp.inf) for s, b in zip(ss, blocks)]

        following = scores(tiles[0])
        for i in tiles:
            ss = following
            if i != tiles[-1]:
                following = scores(i + 1)
            top = ss[0]
            for s in ss[1:]:
                top = jnp.maximum(top, s)
            before = m_s[i]
            now = jnp.maximum(before, jnp.max(top, axis=0, keepdims=True))
            rescale = jnp.exp2((before - now) * C2)
            shift = now * C2
            total = None
            acc = acc_s[i] * rescale
            for s, (n, k, _, vb, _) in zip(ss, blocks):
                p = jnp.exp2(s * C2 - shift)
                total = p if total is None else total + p
                acc = acc + dot(values_of(n, k, vb), p.astype(BF16), NN)
            m_s[i] = now
            l_s[i] = l_s[i] * rescale + jnp.sum(total, axis=0, keepdims=True)
            acc_s[i] = acc

    def prefix(n):
        live = off_ref[0]
        return [(n, k, CK, CV, lambda half, k=k: key_row < live - (2 * n + k) * 256) for k in (0, 1)]

    def stretch(n):
        return [(n, k, SK, SV, None) for k in (0, 1)]

    def diagonal():
        def until(k):
            return lambda half: key_row + (k - core) * 256 <= query_row + half * 128

        return [(z, k, SK, SV, until(k)) for k in (0, 1)]

    def visible(tiles, k):
        @pl.when((z >= k) & (z + k >= CHIPS))
        def _():
            attend(tiles, stretch(z - k) + stretch(z + k - CHIPS))

        @pl.when((z >= k) & (z + k < CHIPS))
        def _():
            attend(tiles, stretch(z - k))

    def farthest(tiles, k):
        live = off_ref[0]
        cached_block = (far, k, CK, CV, lambda half: key_row < live - (2 * far + k) * 256)

        @pl.when(z >= 4)
        def _():
            attend(tiles, [cached_block, (z - 4, k, SK, SV, None)])

        @pl.when(z < 4)
        def _():
            attend(tiles, [cached_block])

    def settle(half, u):
        for p in (0, 1):
            i = 4 * half + 2 * u + p
            rows = (acc_s[i] / l_s[i]).T.astype(BF16)
            for j in (0, 1):
                abuf[half, z, core, 2 * u + p, :, j * HEAD : (j + 1) * HEAD] = rows[j * 128 : (j + 1) * 128]
            atr[half].begin(2 * u + p)

    y, x = t // 2, lax.rem(t, 2)
    across = (c, t + 1 - 2 * x, g)

    def along(j):
        return (c, lax.rem(y + j, 4) * 2 + x, g)

    def stand_in(buf, send, recv):
        return remote(buf, buf, send, recv, beside)

    def multiply(h, n):
        for u in (0, 1):
            atr[h].from_sib(n, u).wait_recv()
        rows = jnp.concatenate([abuf[h, n, :, u].reshape(256, 256) for u in range(4)], axis=1)
        rows = dot(rows, w_s[...], NN).astype(BF16)
        pbuf[h, n, 0] = rows[:, :256].reshape(4, 2, 32, 256)
        pbuf[h, n, 1] = rows[:, 256:].reshape(4, 2, 32, 256)

    def spread(h, n):
        remote(pbuf.at[h, n, 0, :, 1 - x], xb.at[CHIPS * h + n], gsend.at[0], xrecv.at[h, n], across).start()
        for j in (1, 2, 3):
            to = lax.rem(y + j, 4)
            remote(
                pbuf.at[h, n, 1, to], yb.at[CHIPS * h + n, j - 1], gsend.at[1], yrecv.at[h, n], along(j)
            ).start()

    def project(h, n):
        multiply(h, n)
        spread(h, n)

    def middle(h, n):
        stand_in(xb.at[CHIPS * h + n], gsend.at[0], xrecv.at[h, n]).wait_recv()
        total = pbuf[h, n, 0, :, x].astype(F32) + xb[CHIPS * h + n].astype(F32)
        s0[h, n] = total.astype(BF16)
        for j in (1, 2, 3):
            to = lax.rem(y + j, 4)
            remote(
                s0.at[h, n, to], yb2.at[CHIPS * h + n, j - 1], gsend.at[2], yrecv2.at[h, n], along(j)
            ).start()
        stand_in(yb.at[CHIPS * h + n], gsend.at[1], yrecv.at[h, n]).wait_recv()
        total = pbuf[h, n, 1, y].astype(F32)
        for j in range(3):
            total = total + yb[CHIPS * h + n, j].astype(F32)
        s1[h, n] = total.astype(BF16)
        remote(s1.at[h, n, 1 - x], xb2.at[CHIPS * h + n], gsend.at[3], xrecv2.at[h, n], across).start()

    def collect(h, n):
        stand_in(yb2.at[CHIPS * h + n], gsend.at[2], yrecv2.at[h, n]).wait_recv()
        first = s0[h, n, y].astype(F32)
        for j in range(3):
            first = first + yb2[CHIPS * h + n, j].astype(F32)
        stand_in(xb2.at[CHIPS * h + n], gsend.at[3], xrecv2.at[h, n]).wait_recv()
        second = s1[h, n, x].astype(F32) + xb2[CHIPS * h + n].astype(F32)

        hand_in(h, n, first, second)

    def hand_in(h, n, first, second):
        @pl.when(n == t)
        def _():
            obuf[h, t, 0] = first.astype(BF16)
            obuf[h, t, 1] = second.astype(BF16)

        @pl.when(n != t)
        def _():
            sbuf[h, n, 0] = first.astype(BF16)
            sbuf[h, n, 1] = second.astype(BF16)
            remote(sbuf.at[h, n], obuf.at[h, t], osend.at[h], orecv.at[h], (c, n, g)).start()

    def project_last(k):
        rows = jnp.concatenate([abuf[1, far, k, u] for u in range(4)], axis=1)
        rows = dot(rows, w_s[...], NN).astype(BF16)
        pbuf[1, far, 0, pl.ds(2 * k, 2)] = rows[:, :256].reshape(2, 2, 32, 256)
        pbuf[1, far, 1, pl.ds(2 * k, 2)] = rows[:, 256:].reshape(2, 2, 32, 256)

        def send(j, _):
            to = 4 * k + j

            @pl.when(to != t)
            def _():
                slot = lax.rem(to - t - 1 + TP, TP)
                remote(
                    pbuf.at[1, far, :, to // 2, lax.rem(to, 2)], rb.at[slot], gsend.at[4], rrecv, (c, to, g)
                ).start()

            return 0

        lax.fori_loop(0, 4, send, 0)

    def collect_last():
        stand_in(rb, gsend.at[4], rrecv).wait_recv()
        total = pbuf[1, far, :, y, x].astype(F32)
        for j in range(TP - 1):
            total = total + rb[j].astype(F32)
        hand_in(1, far, total[0], total[1])

    row_id = lax.broadcasted_iota(jnp.int32, (128, 256), 0)
    col_id = lax.broadcasted_iota(jnp.int32, (128, 256), 1)
    request = lax.rem(row_id, 16) // 2

    def fold(state, parts):
        acc, m, l = state[:, 0:128], state[:, 128:129], state[:, 256:257]
        now = m
        for s, _ in parts:
            now = jnp.maximum(now, jnp.max(s, axis=1, keepdims=True))
        rescale = jnp.exp2((m - now) * C2)
        l = l * rescale
        acc = acc * rescale
        for s, weigh in parts:
            p = jnp.exp2((s - now) * C2)
            l = l + jnp.sum(p, axis=1, keepdims=True)
            acc = acc + weigh(p.astype(BF16))
        state[:, 0:128] = acc
        state[:, 128:256] = jnp.broadcast_to(now, (128, 128))
        state[:, 256:384] = jnp.broadcast_to(l, (128, 128))

    def hand_over(first, last):
        wanted = (request + c * 8).astype(F32)

        def one(n, _):
            parts = []
            for k in (0, 1):
                labels = kv[n, k, LB : LB + 16, :].astype(F32)
                label = jnp.concatenate([labels[0:1], labels[1:2]], axis=1)
                s = dot(dqp[...], kv[n, k, SK : SK + 256, :], NT)
                s = jnp.where(label == wanted, s, -jnp.inf)
                parts.append((s, lambda p, k=k: dot(p, values_of(n, k, SV), NT)))
            fold(hand, parts)
            return 0

        lax.fori_loop(first, last, one, 0)

    def cached(first, last):
        def one(i, _):
            parts = []
            for k in (0, 1):
                r = 2 * i + k
                rows = pl.ds(pl.multiple_of(r * 256, 256), 256)
                s = dot(dqs[...], dck_s[rows, :], NT)
                s = jnp.where((request == r) & (col_id < len_ref[r]), s, -jnp.inf)
                parts.append((s, lambda p, rows=rows: dot(p, dcv_s[rows, :], NN)))
            fold(own, parts)
            return 0

        lax.fori_loop(first, last, one, 0)

    def fresh():
        rows16 = lax.broadcasted_iota(jnp.int32, (128, 16), 0)
        cols16 = lax.broadcasted_iota(jnp.int32, (128, 16), 1)
        seen = (lax.rem(rows16, 16) // 2 == cols16 // 2) & (lax.rem(cols16, 2) <= lax.rem(rows16, 2))
        s = jnp.where(seen, dot(dqs[...], dk_s[...], NT), -jnp.inf)
        fold(own, [(s, lambda p: dot(p, dv_s[...], NN))])

    hand_copy = remote(hand, handin, hsend, hrecv, other)

    early, late = range(0, 5), range(5, 8)
    for u in (0, 1):
        kvr.from_sib(z, u).wait_recv()
    attend(early, prefix(z) + diagonal())

    def kv_step(k, _):
        before, after = chip(z - k), chip(z + k)
        kvr.event(k, 0)

        @pl.when(k > 1)
        def _():
            kvr.from_sib(chip(z - k + 1), 1).wait_recv()
            kvr.from_sib(chip(z + k - 1), 1).wait_recv()
            visible(early, k - 1)

        kvr.event(k, 1)
        kvr.from_sib(before, 0).wait_recv()
        kvr.from_sib(after, 0).wait_recv()
        attend(early, prefix(before) + prefix(after))
        return 0

    lax.fori_loop(1, 4, kv_step, 0)
    kvr.last(0)
    kvr.from_sib(chip(z - 3), 1).wait_recv()
    kvr.from_sib(chip(z + 3), 1).wait_recv()
    visible(early, 3)
    kvr.last(1)
    farthest(early, core)
    kvr.from_sib(far, 0).wait_recv()
    kvr.from_sib(far, 1).wait_recv()
    farthest((0, 1), 1 - core)
    settle(0, 0)
    farthest((2, 3), 1 - core)
    settle(0, 1)

    farthest((4,), 1 - core)
    attend(late, prefix(z) + diagonal())
    ins[6].wait()

    def first_step(k, _):
        before, after = chip(z - k), chip(z + k)
        atr[0].event(k, 0)
        visible(late, k)

        @pl.when(k == 1)
        def _():
            project(0, z)

        @pl.when(k > 1)
        def _():
            project(0, chip(z - k + 1))

        @pl.when(k == 2)
        def _():
            middle(0, z)

        @pl.when(k == 3)
        def _():
            middle(0, chip(z - 1))
            collect(0, z)

        atr[0].event(k, 1)
        attend(late, prefix(before) + prefix(after))

        @pl.when(k > 1)
        def _():
            project(0, chip(z + k - 1))

        @pl.when(k == 3)
        def _():
            middle(0, chip(z + 1))

        return 0

    lax.fori_loop(1, 4, first_step, 0)
    @pl.when(z >= 4)
    def _():
        attend(late, prefix(far) + stretch(z - 4))

    @pl.when(z < 4)
    def _():
        attend(late, prefix(far))

    settle(1, 0)
    settle(1, 1)
    atr[0].last(0)
    atr[0].last(1)
    project(0, chip(z - 3))
    project(0, chip(z + 3))
    middle(0, chip(z - 2))
    middle(0, chip(z + 2))
    project(0, far)
    project(1, z)
    dq_copy.wait_recv()
    for i in range(7, 11):
        ins[i].wait()

    def second_step(k, _):
        before, after = chip(z - k), chip(z + k)
        atr[1].event(k, 0)

        @pl.when(k == 1)
        def _():
            collect(0, chip(z - 1))
            collect(0, chip(z + 1))
            hand_over(0, 2)

        @pl.when(k == 2)
        def _():
            collect(0, chip(z - 2))
            collect(0, chip(z + 2))
            hand_over(5, 7)

        @pl.when(k == 3)
        def _():
            collect(0, chip(z - 3))
            collect(0, chip(z + 3))
            cached(0, 2)

        atr[1].event(k, 1)
        project(1, before)
        project(1, after)

        @pl.when(k == 1)
        def _():
            middle(0, chip(z - 3))
            middle(0, chip(z + 3))
            middle(0, far)
            middle(1, z)
            hand_over(2, 5)

        @pl.when(k == 2)
        def _():
            middle(1, chip(z - 1))
            middle(1, chip(z + 1))
            hand_over(7, 8)
            hand_copy.start()

        @pl.when(k == 3)
        def _():
            middle(1, chip(z - 2))
            middle(1, chip(z + 2))
            collect(0, far)
            collect(1, z)
            collect(1, chip(z - 1))
            collect(1, chip(z + 1))

        return 0

    def sums(h):
        seven = obuf.at[h, pl.ds(0, TP - 1)]
        return remote(seven, seven, osend.at[h], orecv.at[h], beside)

    def deliver(h):
        sums(h).wait_recv()
        for j in range(TP):
            first = j // 4 * 256 + h * 128 + j % 4 * 32
            for half in (0, 1):
                out_ref[first : first + 32, half * 256 : (half + 1) * 256] = obuf[h, j, half]

    lax.fori_loop(1, 4, second_step, 0)
    cached(2, 4)
    atr[1].last(0)
    atr[1].last(1)
    project_last(core)
    middle(1, chip(z - 3))
    middle(1, chip(z + 3))
    for v in (0, 1):
        atr[1].from_sib(far, v).wait_recv()
    project_last(1 - core)
    collect(1, chip(z - 2))
    collect(1, chip(z + 2))
    fresh()

    hand_copy.wait_recv()
    m, l = own[:, 128:129], own[:, 256:257]
    m_h, l_h = handin[:, 128:129], handin[:, 256:257]
    top = jnp.maximum(m, m_h)
    a, b = jnp.exp2((m - top) * C2), jnp.exp2((m_h - top) * C2)
    result = (own[:, 0:128] * a + handin[:, 0:128] * b) / (l * a + l_h * b)
    for h in range(HEADS):
        dec_ref[:, :, h * HEAD : (h + 1) * HEAD] = result[h * 16 : (h + 1) * 16].reshape(8, 2, HEAD).astype(BF16)
    collect(1, chip(z - 3))
    collect(1, chip(z + 3))
    collect_last()

    dq_copy.wait_send()
    hand_copy.wait_send()
    kvr.drain(lambda ns: kv.at[ns, 0])
    for h in (0, 1):
        atr[h].drain(lambda ns, h=h: abuf.at[h, ns, 0])
    deliver(0)
    for i, buf in enumerate((xb, yb, yb2, xb2)):
        most = buf.at[pl.ds(0, 2 * CHIPS - 1)]
        stand_in(most, gsend.at[i], gsend.at[i]).wait_send()
    stand_in(rb, gsend.at[4], rrecv).wait_send()
    deliver(1)
    for h in (0, 1):
        sums(h).wait_send()


def shards(
    pre_q, pre_k, pre_v, pre_ck, pre_cv, tract_offset, owner, tag, out_weight,
    dec_q, dec_k, dec_v, dec_ck, dec_cv, cache_len,
):
    vmem, dma = pltpu.VMEM, pltpu.SemaphoreType.DMA
    anywhere = pl.BlockSpec(memory_space=pl.ANY)
    smem = pl.BlockSpec(memory_space=pltpu.SMEM)
    whole = pl.BlockSpec(memory_space=pltpu.VMEM)
    out, dec = pl.pallas_call(
        kernel,
        out_shape=(jax.ShapeDtypeStruct((512, 512), BF16), jax.ShapeDtypeStruct((8, 2, 1024), BF16)),
        in_specs=[smem, smem, whole, whole] + [anywhere] * 11,
        out_specs=(whole, whole),
        scratch_shapes=[
            vmem((CHIPS, 2, PACK, HEAD), BF16),
            vmem((ROWS, 1024), BF16),
            vmem((HEADS, 256, HEAD), BF16),
            vmem((2, ROWS, HEAD), BF16),
            vmem((1024, 512), BF16),
            vmem((8, 2, 1024), BF16),
            vmem((128, HEAD), BF16),
            vmem((16, HEAD), BF16),
            vmem((16, HEAD), BF16),
            vmem((2048, HEAD), BF16),
            vmem((2048, HEAD), BF16),
            vmem((HEADS, 1, ROWS), F32),
            vmem((HEADS, 1, ROWS), F32),
            vmem((HEADS, HEAD, ROWS), F32),
            vmem((2, CHIPS, 2, 4, 128, 256), BF16),
            vmem((2, CHIPS, 2, 4, 2, 32, 256), BF16),
            vmem((2 * CHIPS, 4, 32, 256), BF16),
            vmem((2 * CHIPS, 3, 2, 32, 256), BF16),
            vmem((2, CHIPS, 4, 32, 256), BF16),
            vmem((2, CHIPS, 2, 32, 256), BF16),
            vmem((2 * CHIPS, 32, 256), BF16),
            vmem((2 * CHIPS, 3, 32, 256), BF16),
            vmem((TP - 1, 2, 32, 256), BF16),
            vmem((2, CHIPS, 2, 32, 256), BF16),
            vmem((2, TP, 2, 32, 256), BF16),
            vmem((128, HEAD), BF16),
            vmem((128, 384), F32),
            vmem((128, 384), F32),
            vmem((128, 384), F32),
            dma((11,)),
            dma, dma((2, 4, 4)), dma, dma((CHIPS, 2)),
            dma((2,)), dma((4, 4, 4)), dma((2,)), dma((4, CHIPS)),
            dma((5,)), dma((2, CHIPS)), dma((2, CHIPS)), dma((2, CHIPS)), dma((2, CHIPS)), dma, dma((2,)), dma((2,)),
            dma, dma, dma, dma,
        ],
        compiler_params=pltpu.CompilerParams(
            collective_id=0, has_side_effects=True, vmem_limit_bytes=56 << 20
        ),
        cost_estimate=pl.CostEstimate(flops=14 << 30, bytes_accessed=6 << 20, transcendentals=17 << 20),
    )(
        tract_offset,
        cache_len[0],
        owner.reshape(1, ROWS),
        tag,
        pre_q[0],
        pre_k[0],
        pre_v[0],
        pre_ck[0],
        pre_cv[0],
        out_weight,
        dec_q[0],
        dec_k.reshape(16, HEAD),
        dec_v.reshape(16, HEAD),
        dec_ck.reshape(2048, HEAD),
        dec_cv.reshape(2048, HEAD),
    )
    return out[None], dec[None]


def solution(mesh):
    return jax.shard_map(
        shards,
        mesh=mesh,
        in_specs=(
            P("grp", "ctx", "tp"),
            P("grp", "ctx", "tp"),
            P("grp", "ctx", "tp"),
            P("grp", "ctx", "tp"),
            P("grp", "ctx", "tp"),
            P("grp"),
            P("grp", "ctx", None),
            P("grp", "ctx"),
            P("tp", "ctx"),
            P("grp", "ctx", None, "tp"),
            P("grp", "ctx", None, "tp"),
            P("grp", "ctx", None, "tp"),
            P("grp", "ctx", None, "tp"),
            P("grp", "ctx", None, "tp"),
            P("grp", "ctx"),
        ),
        out_specs=(P("grp", "tp", "ctx"), P("grp", "ctx", None, "tp")),
        check_vma=False,
    )
```
